128 devices in a mesh: dp: 2 (over core), blk: 16 (over z, y), heads: 4 (over x).
Axes of the slice: x: 4, y: 4, z: 4, core: 2. Of those that a mesh axis runs over, the one named last changes fastest.
Arguments:
- inputs: bfloat16 [16384, 768], P(('dp', 'blk', 'heads')), may hold values from -6 to 6
- cotangent: bfloat16 [16384, 768], P(('dp', 'blk', 'heads')), may hold values from -6 to 6
- qkv_weight: float32 [768, 2304], P(('dp', 'blk', 'heads')), may hold values from -0.3125 to 0.3125
- attn_weight: float32 [768, 768], P(('dp', 'blk', 'heads')), may hold values from -0.875 to 0.875
- up_weight: float32 [768, 3072], P(('dp', 'blk', 'heads')), may hold values from -0.21875 to 0.21875
- down_weight: float32 [3072, 768], P(('dp', 'blk', 'heads')), may hold values from -0.109375 to 0.109375
- vectors: float32 [12, 768], P(None, ('dp', 'blk', 'heads')), as said below
- qkv_first: float32 [768, 2304], P(('dp', 'blk', 'heads')), as said below
- attn_first: float32 [768, 768], P(('dp', 'blk', 'heads')), as said below
- up_first: float32 [768, 3072], P(('dp', 'blk', 'heads')), as said below
- down_first: float32 [3072, 768], P(('dp', 'blk', 'heads')), as said below
- vector_first: float32 [12, 768], P(None, ('dp', 'blk', 'heads')), as said below
- qkv_second: float32 [768, 2304], P(('dp', 'blk', 'heads')), as said below
- attn_second: float32 [768, 768], P(('dp', 'blk', 'heads')), as said below
- up_second: float32 [768, 3072], P(('dp', 'blk', 'heads')), as said below
- down_second: float32 [3072, 768], P(('dp', 'blk', 'heads')), as said below
- vector_second: float32 [12, 768], P(None, ('dp', 'blk', 'heads')), as said below
Outputs:
- output: bfloat16 [16384, 768], P(('dp', 'blk', 'heads'))
- input_grad: float32 [16384, 768], P(('dp', 'blk', 'heads'))
- qkv_updated: float32 [768, 2304], P(('dp', 'blk', 'heads'))
- attn_updated: float32 [768, 768], P(('dp', 'blk', 'heads'))
- up_updated: float32 [768, 3072], P(('dp', 'blk', 'heads'))
- down_updated: float32 [3072, 768], P(('dp', 'blk', 'heads'))
- vector_updated: float32 [12, 768], P(None, ('dp', 'blk', 'heads'))
- qkv_moment: float32 [768, 2304], P(('dp', 'blk', 'heads'))
- attn_moment: float32 [768, 768], P(('dp', 'blk', 'heads'))
- up_moment: float32 [768, 3072], P(('dp', 'blk', 'heads'))
- down_moment: float32 [3072, 768], P(('dp', 'blk', 'heads'))
- vector_moment: float32 [12, 768], P(None, ('dp', 'blk', 'heads'))
- qkv_squares: float32 [768, 2304], P(('dp', 'blk', 'heads'))
- attn_squares: float32 [768, 768], P(('dp', 'blk', 'heads'))
- up_squares: float32 [768, 3072], P(('dp', 'blk', 'heads'))
- down_squares: float32 [3072, 768], P(('dp', 'blk', 'heads'))
- vector_squares: float32 [12, 768], P(None, ('dp', 'blk', 'heads'))
The draws below stay inside these ranges and needn't reach their ends.
Inputs may be any that keep to these rules, and one draw needn't show every extreme that they name: `vectors`: rows 0 and 5 lie in 0.6 to 1.4; the other rows have a spread of about 0.2 with both signs. `qkv_first`: both signs. `attn_first`: both signs. `up_first`: both signs. `down_first`: both signs. `vector_first`: both signs. `qkv_second`: positive. `attn_second`: positive. `up_second`: positive. `down_second`: positive. `vector_second`: positive.
All inputs are finite; a program needn't handle non-finite values.
Results may differ from the reference program's by a relative error of at most 0.028.
Values may be sent and summed in bfloat16 or wider, within the bound.
No kernel may reach another device: no remote copies, remote signals or barrier semaphores. Data moves between devices by JAX's collectives and lax.ppermute only.
A program may use at most 128 MiB of HBM per device.

```python
import math
import jax
import jax.numpy as jnp
from jax import lax

D = 768
HEADS = 12
FF = 3072
HEAD_DIM = 64
STEP = 10
SEQ = 8192
TOKENS = 16384
N_DP = 2


def first_moment(seed_key, extent, grad_size):
    return grad_size * 0.1 / 0.9 * jax.random.normal(seed_key, extent, jnp.float32)


def second_moment(seed_key, extent, grad_size):
    baseline = 0.05 / 0.95 * grad_size * grad_size
    return baseline * jax.random.uniform(seed_key, extent, jnp.float32, 1.0, 4.0)


def draw_vectors(key, part):
    key = jax.random.fold_in(key, 3)
    gains = jax.random.uniform(key, (12, D), jnp.float32, 0.6, 1.4)
    shifts = 0.2 * jax.random.normal(jax.random.fold_in(key, 1), (12, D), jnp.float32)
    row_index = lax.iota(jnp.int32, 12)
    is_gain = (row_index == 0) | (row_index == 5)
    return jnp.where(is_gain[:, None], gains, shifts)


def draw_qkv_first(key, part):
    key = jax.random.fold_in(key, 11)
    return first_moment(key, (D, 3 * D), 1.5 * math.sqrt(TOKENS))


def draw_attn_first(key, part):
    key = jax.random.fold_in(key, 12)
    return first_moment(key, (D, D), 0.5 * math.sqrt(TOKENS))


def draw_up_first(key, part):
    key = jax.random.fold_in(key, 13)
    return first_moment(key, (D, FF), 0.3 * math.sqrt(TOKENS))


def draw_down_first(key, part):
    key = jax.random.fold_in(key, 14)
    return first_moment(key, (FF, D), 0.65 * math.sqrt(TOKENS))


def draw_vector_first(key, part):
    key = jax.random.fold_in(key, 15)
    return first_moment(key, (12, D), math.sqrt(TOKENS))


def draw_qkv_second(key, part):
    key = jax.random.fold_in(key, 21)
    return second_moment(key, (D, 3 * D), 1.5 * math.sqrt(TOKENS))


def draw_attn_second(key, part):
    key = jax.random.fold_in(key, 22)
    return second_moment(key, (D, D), 0.5 * math.sqrt(TOKENS))


def draw_up_second(key, part):
    key = jax.random.fold_in(key, 23)
    return second_moment(key, (D, FF), 0.3 * math.sqrt(TOKENS))


def draw_down_second(key, part):
    key = jax.random.fold_in(key, 24)
    return second_moment(key, (FF, D), 0.65 * math.sqrt(TOKENS))


def draw_vector_second(key, part):
    key = jax.random.fold_in(key, 25)
    return second_moment(key, (12, D), math.sqrt(TOKENS))


def block_scale(own_key, dims, cuts, least, largest):
    level, own = 1.0, jax.random.fold_in(own_key, 6)
    for axis_at, parts in cuts:
        steps = jnp.exp(jax.random.uniform(jax.random.fold_in(own, axis_at), (parts,), jnp.float32, least / len(cuts), largest / len(cuts)))
        level = level * jnp.repeat(steps, dims[axis_at] // parts).reshape([-1 if axis == axis_at else 1 for axis in range(len(dims))])
    return level


def scatter_about(rng, shape, width, bound, split=(), kind=jnp.bfloat16):
    values = jax.random.normal(rng, shape, jnp.float32) * width
    if len(split) > 0:
        values = block_scale(rng, shape, split, -0.22, 0.18) * values
    return jnp.clip(values, min=-bound, max=bound).astype(kind)


def setup_inputs(seed: int = 0) -> dict:
    key_of = jax.random.split(jax.random.key(seed), 18)
    inputs = scatter_about(key_of[0], (TOKENS, D), 1.0, 6.0, ((0, 128),))
    cotangent = scatter_about(key_of[1], (TOKENS, D), 1.0, 6.0, ((0, 128),))
    qkv_weight = scatter_about(key_of[2], (D, 3 * D), (D // 2) ** -0.5, 0.3125, ((0, 128),), jnp.float32)
    attn_weight = scatter_about(key_of[3], (D, D), (D // 16) ** -0.5, 0.875, ((0, 128),), jnp.float32)
    up_weight = scatter_about(key_of[4], (D, FF), D ** -0.5, 0.21875, ((0, 128),), jnp.float32)
    down_weight = scatter_about(key_of[5], (FF, D), FF ** -0.5, 0.109375, ((0, 128),), jnp.float32)
    vectors = draw_vectors(jax.random.fold_in(key_of[17], 71), 0)
    qkv_first = draw_qkv_first(jax.random.fold_in(key_of[17], 71), 0)
    attn_first = draw_attn_first(jax.random.fold_in(key_of[17], 71), 0)
    up_first = draw_up_first(jax.random.fold_in(key_of[17], 71), 0)
    down_first = draw_down_first(jax.random.fold_in(key_of[17], 71), 0)
    vector_first = draw_vector_first(jax.random.fold_in(key_of[17], 71), 0)
    qkv_second = draw_qkv_second(jax.random.fold_in(key_of[17], 71), 0)
    attn_second = draw_attn_second(jax.random.fold_in(key_of[17], 71), 0)
    up_second = draw_up_second(jax.random.fold_in(key_of[17], 71), 0)
    down_second = draw_down_second(jax.random.fold_in(key_of[17], 71), 0)
    vector_second = draw_vector_second(jax.random.fold_in(key_of[17], 71), 0)
    return dict(inputs=inputs, cotangent=cotangent, qkv_weight=qkv_weight, attn_weight=attn_weight, up_weight=up_weight, down_weight=down_weight, vectors=vectors, qkv_first=qkv_first, attn_first=attn_first, up_first=up_first, down_first=down_first, vector_first=vector_first, qkv_second=qkv_second, attn_second=attn_second, up_second=up_second, down_second=down_second, vector_second=vector_second)


@jax.custom_vjp
def low(v):
    return lax.optimization_barrier(v.astype(jnp.bfloat16)).astype(jnp.float32)

@jax.custom_vjp
def low_back(v):
    return v

def low_keep(v):
    return (low(v), None)

def low_pass(kept, grad):
    return (grad,)

def back_keep(v):
    return (v, None)

def back_low(kept, grad):
    return (low(grad),)
low.defvjp(low_keep, low_pass)
low_back.defvjp(back_keep, back_low)
norm_epsilon = 1e-05
first_decay = 0.9
second_decay = 0.95
adam_epsilon = 1e-08
weight_decay = 0.1
learning_rates = (0.04, 0.1, 0.03, 0.02, 0.7)
decay_flags = (1.0, 1.0, 1.0, 1.0, 0.0)
masked_score = -1e+30
highest = lax.Precision.HIGHEST

def layer_norm(values, gain, shift):
    centred = values - lax.optimization_barrier(jnp.mean(values, axis=-1, keepdims=True))
    variance = lax.optimization_barrier(jnp.mean(centred * centred, axis=-1, keepdims=True))
    return centred * lax.rsqrt(variance + norm_epsilon) * gain + shift

def attend_block(query_block, first_row, seq_keys, seq_values):
    scaling = HEAD_DIM ** (-0.5)
    scores = jnp.einsum('qhd,khd->hqk', query_block, seq_keys, precision=highest) * scaling
    scores = low_back(scores)
    query_places = first_row + lax.iota(jnp.int32, query_block.shape[0])
    key_places = lax.iota(jnp.int32, seq_keys.shape[0])
    allowed = key_places[None, :] <= query_places[:, None]
    scores = jnp.where(allowed[None], scores, masked_score)
    row_peak = lax.optimization_barrier(jnp.max(scores, axis=-1, keepdims=True))
    raised = jnp.exp(scores - row_peak)
    weights = low(raised / lax.optimization_barrier(jnp.sum(raised, axis=-1, keepdims=True)))
    return jnp.einsum('hqk,khd->qhd', weights, seq_values, precision=highest)

def attention(mixed_rows):
    grouped = mixed_rows.reshape(N_DP, SEQ, 3, HEADS, HEAD_DIM)
    block_rows = math.gcd(SEQ, 256)
    block_count = SEQ // block_rows
    firsts = lax.iota(jnp.int32, block_count) * block_rows
    checked = jax.checkpoint(attend_block)
    results = []
    for sequence in range(N_DP):
        seq_keys = grouped[sequence, :, 1]
        seq_values = grouped[sequence, :, 2]
        query_blocks = grouped[sequence, :, 0].reshape(block_count, block_rows, HEADS, HEAD_DIM)

        def one_block(block_pair):
            return checked(block_pair[0], block_pair[1], seq_keys, seq_values)
        results.append(lax.map(one_block, (query_blocks, firsts)).reshape(SEQ, D))
    return jnp.concatenate(results, axis=0)

def forward(inputs, qkv_weight, attn_weight, up_weight, down_weight, vectors):
    qkv_copy = low(qkv_weight)
    attn_copy = low(attn_weight)
    up_copy = low(up_weight)
    down_copy = low(down_weight)
    vector_copy = low(vectors)
    normed_one = low(layer_norm(inputs, vector_copy[0], vector_copy[1]))
    bias_row = jnp.concatenate([vector_copy[2], jnp.zeros_like(vector_copy[2]), vector_copy[3]])
    mixed_rows = low(low_back(jnp.dot(normed_one, qkv_copy, precision=highest) + bias_row))
    attended = low(low_back(attention(mixed_rows)))
    branch = low_back(jnp.dot(attended, attn_copy, precision=highest) + vector_copy[4])
    residual = inputs + branch
    normed_two = low(layer_norm(residual, vector_copy[5], vector_copy[6]))
    hidden_pre = low_back(jnp.dot(normed_two, up_copy, precision=highest) + vector_copy[8:12].reshape(FF))
    hidden = low(jax.nn.gelu(hidden_pre, approximate=True))
    return residual + jnp.dot(hidden, down_copy, precision=highest) + vector_copy[7]

def adam_step(weight, gradient, first, second, rate, decay_flag):
    moment = first_decay * first + (1.0 - first_decay) * gradient
    squares = second_decay * second + (1.0 - second_decay) * gradient * gradient
    fix_one = 1.0 - first_decay ** STEP
    fix_two = 1.0 - second_decay ** STEP
    direction = moment / fix_one / (jnp.sqrt(squares / fix_two) + adam_epsilon)
    updated = weight - rate * (direction + decay_flag * weight_decay * weight)
    return (updated, moment, squares)

def reference(inputs, cotangent, qkv_weight, attn_weight, up_weight, down_weight, vectors, qkv_first, attn_first, up_first, down_first, vector_first, qkv_second, attn_second, up_second, down_second, vector_second):
    masters = (qkv_weight, attn_weight, up_weight, down_weight, vectors)
    firsts = (qkv_first, attn_first, up_first, down_first, vector_first)
    seconds = (qkv_second, attn_second, up_second, down_second, vector_second)
    result, pullback = jax.vjp(forward, inputs.astype(jnp.float32), *masters)
    gradients = pullback(cotangent.astype(jnp.float32))
    updates = []
    for member in range(5):
        updates.append(adam_step(masters[member], gradients[member + 1], firsts[member], seconds[member], learning_rates[member], decay_flags[member]))
    return (result.astype(jnp.bfloat16), gradients[0], updates[0][0], updates[1][0], updates[2][0], updates[3][0], updates[4][0], updates[0][1], updates[1][1], updates[2][1], updates[3][1], updates[4][1], updates[0][2], updates[1][2], updates[2][2], updates[3][2], updates[4][2])
```

```python
import functools

import jax
import jax.numpy as jnp
from jax import lax
from jax.experimental import pallas as pl
from jax.experimental.pallas import tpu as pltpu
from jax.sharding import PartitionSpec as P

STEP = 10
WIDTH = 768
HIDDEN = 3072
HEAD_DIM = 64
GROUPS = 4
GROUP_HEADS = 3
GROUP_WIDTH = 192
BLOCKS = 16
QUARTERS = 4
TOKENS = 128
BLOCK_ROWS = 512
OWNERS = 128
QUERY_TILE = 256
QUERY_ROWS = BLOCKS * TOKENS
TILES = QUERY_ROWS // QUERY_TILE
EVERY = ("dp", "blk", "heads")

norm_epsilon = 1e-05
first_decay = 0.9
second_decay = 0.95
adam_epsilon = 1e-08
weight_decay = 0.1
masked_score = -1e30
bf16 = jnp.bfloat16
f32 = jnp.float32


def shifted(array, axis, by):
    count = lax.axis_size(axis)
    return lax.ppermute(array, axis, [(i, (i + by) % count) for i in range(count)])


def gather_slots(array):
    return [array] + [shifted(array, "heads", by) for by in range(1, GROUPS)]


def return_slots(slots):
    return [slots[0]] + [shifted(slots[by], "heads", -by) for by in range(1, GROUPS)]


def dot(left, right, left_dim=1, right_dim=0):
    return lax.dot_general(
        left, right, (((left_dim,), (right_dim,)), ((), ())), preferred_element_type=f32
    )


def unit_norm(values):
    centred = values - jnp.mean(values, axis=-1, keepdims=True)
    variance = jnp.mean(centred * centred, axis=-1, keepdims=True)
    inverse = lax.rsqrt(variance + norm_epsilon)
    return centred * inverse, inverse


def norm_backward(grad_rows, unit_rows, inverse, gain):
    scaled = grad_rows * gain
    mean_grad = jnp.mean(scaled, axis=-1, keepdims=True)
    mean_unit = jnp.mean(scaled * unit_rows, axis=-1, keepdims=True)
    return inverse * (scaled - mean_grad - unit_rows * mean_unit)


def call(kernel, outs, scratch=(), smem=0, inputs=0):
    in_specs = [pl.BlockSpec(memory_space=pltpu.SMEM)] * smem + [
        pl.BlockSpec(memory_space=pltpu.VMEM)
    ] * inputs
    return pl.pallas_call(
        kernel,
        out_shape=[jax.ShapeDtypeStruct(shape, dtype) for shape, dtype in outs],
        in_specs=in_specs,
        out_specs=[pl.BlockSpec(memory_space=pltpu.VMEM)] * len(outs),
        scratch_shapes=list(scratch),
        compiler_params=pltpu.CompilerParams(vmem_limit_bytes=56 * 2**20),
    )


def fold_rows(rows):
    return jnp.concatenate([rows[:64], rows[64:]], axis=1)


def unfold_rows(folded):
    return jnp.concatenate([folded[:, :64], folded[:, 64:]], axis=0)


def project_kernel(x0, x1, x2, x3, params, weight, bias, out):
    rows = jnp.concatenate([x0[...], x1[...], x2[...], x3[...]], axis=0).astype(f32)
    unit, _ = unit_norm(rows)
    normed = (unit * params[0:1] + params[1:2]).astype(bf16)
    mixed = (dot(normed, weight[...]) + bias[...]).astype(bf16)
    for head in range(GROUP_HEADS):
        pair = mixed[:, head * 128 : (head + 1) * 128]
        first = 384 + head * HEAD_DIM
        queries = mixed[:, first : first + HEAD_DIM]
        for quarter in range(QUARTERS):
            place = head * QUARTERS + quarter
            out[place, 0:BLOCK_ROWS] = pair
            out[place, BLOCK_ROWS:] = fold_rows(queries[quarter * TOKENS : (quarter + 1) * TOKENS])
    out[GROUP_HEADS * QUARTERS :] = jnp.zeros((BLOCKS - GROUP_HEADS * QUARTERS, 576, 128), bf16)


def places_allowed(scalars, offset):
    member, quarter = scalars[0], scalars[1]
    key_row = lax.broadcasted_iota(jnp.int32, (BLOCK_ROWS, QUERY_TILE), 0)
    query_row = lax.broadcasted_iota(jnp.int32, (BLOCK_ROWS, QUERY_TILE), 1)
    key_sub = (member - key_row // TOKENS + GROUPS) & (GROUPS - 1)
    key_place = offset * BLOCK_ROWS + key_sub * TOKENS + (key_row & (TOKENS - 1))
    query_sub = (member - quarter + GROUPS) & (GROUPS - 1)
    query_place = (
        (query_row // TOKENS) * BLOCK_ROWS + query_sub * TOKENS + (query_row & (TOKENS - 1))
    )
    return key_place <= query_place


def transposed(values):
    return jnp.transpose(values.astype(f32), (1, 0))


def attend_kernel(scalars, arrived, out, out_cols, log_total, query_cols, value_cols):
    for block in range(BLOCKS):
        queries = unfold_rows(arrived[block, BLOCK_ROWS:])
        query_cols[:, block * TOKENS : (block + 1) * TOKENS] = (
            transposed(queries) * 0.125
        ).astype(bf16)
        value_cols[block, 0:64] = transposed(arrived[block, 0:BLOCK_ROWS])[64:128].astype(bf16)
        value_cols[block, 64:80] = jnp.ones((16, BLOCK_ROWS), bf16)

    def tile(step, nothing):
        at = pl.multiple_of(step * QUERY_TILE, QUERY_TILE)
        queries = query_cols[:, pl.ds(at, QUERY_TILE)]

        def visit(block, carried, allowed=None):
            peak, total = carried
            scores = dot(arrived[block, 0:BLOCK_ROWS, 0:64], queries)
            if allowed is not None:
                scores = jnp.where(allowed, scores, masked_score)
            new_peak = jnp.maximum(peak, jnp.max(scores, axis=0, keepdims=True))
            weights = jnp.exp(scores - new_peak).astype(bf16)
            total = total * jnp.exp(peak - new_peak) + dot(value_cols[block], weights)
            return new_peak, total

        carried = (
            jnp.full((1, QUERY_TILE), masked_score, f32),
            jnp.zeros((80, QUERY_TILE), f32),
        )
        carried = visit(2 * step, carried, places_allowed(scalars, 0))
        carried = visit(2 * step + 1, carried, places_allowed(scalars, 1))
        peak, total = lax.fori_loop(0, 2 * step, visit, carried)
        row_total = total[64:65]
        attended = total[0:64] / row_total
        out_cols[:, pl.ds(at, QUERY_TILE)] = attended
        log_total[:, pl.ds(at, QUERY_TILE)] = peak + jnp.log(row_total)
        attended_rows = transposed(attended).astype(bf16)
        out[2 * step] = fold_rows(attended_rows[0:TOKENS])
        out[2 * step + 1] = fold_rows(attended_rows[TOKENS:])
        return nothing

    lax.fori_loop(0, TILES, tile, 0)


def split_three(values):
    high = values.astype(bf16)
    rest = values - high.astype(f32)
    middle = rest.astype(bf16)
    low = (rest - middle.astype(f32)).astype(bf16)
    return high, middle, low


def attend_back_kernel(
    scalars,
    arrived,
    grads,
    out_cols,
    log_total,
    out,
    query_cols,
    grad_cols,
    query_rows,
    grad_rows,
    key_cols,
    query_total,
    pair_total,
):
    key_lane = lax.broadcasted_iota(jnp.int32, (BLOCK_ROWS, 128), 1)
    zeros = jnp.zeros((TOKENS, 64), bf16)
    lane_row = lax.broadcasted_iota(jnp.int32, (64, TOKENS), 0)
    for block in range(BLOCKS):
        here = slice(block * TOKENS, (block + 1) * TOKENS)
        queries = unfold_rows(arrived[block, BLOCK_ROWS:]) * 0.125
        query_rows[here] = jnp.concatenate([queries, zeros], axis=1)
        query_cols[0:64, here] = transposed(queries).astype(bf16)
        parts = split_three(-log_total[:, here])
        query_cols[64:128, here] = jnp.where(
            lane_row == 0,
            parts[0].astype(f32),
            jnp.where(
                lane_row == 1,
                parts[1].astype(f32),
                jnp.where(lane_row == 2, parts[2].astype(f32), 0.0),
            ),
        ).astype(bf16)
        out_grad = unfold_rows(grads[block])
        grad_rows[here] = jnp.concatenate([zeros, out_grad], axis=1)
        grad_col = transposed(out_grad)
        grad_cols[64:128, here] = grad_col.astype(bf16)
        delta = jnp.sum(grad_col * out_cols[:, here], axis=0, keepdims=True)
        parts = split_three(-delta)
        grad_cols[0:64, here] = jnp.where(
            lane_row == 0,
            parts[0].astype(f32),
            jnp.where(
                lane_row == 1,
                parts[1].astype(f32),
                jnp.where(lane_row == 2, parts[2].astype(f32), 0.0),
            ),
        ).astype(bf16)
        key_cols[block] = transposed(arrived[block, 0:BLOCK_ROWS])[0:64].astype(bf16)
    query_total[...] = jnp.zeros((64, QUERY_ROWS), f32)

    def key_block(block, nothing):
        pair = arrived[block, 0:BLOCK_ROWS]
        keys = jnp.where(key_lane < 64, pair, jnp.where(key_lane < 67, 1.0, 0.0).astype(bf16))
        values = jnp.where(key_lane >= 64, pair, jnp.where(key_lane < 3, 1.0, 0.0).astype(bf16))
        pair_total[...] = jnp.zeros((BLOCK_ROWS, 128), f32)

        def tile(step, nothing, allowed=None):
            at = pl.multiple_of(step * QUERY_TILE, QUERY_TILE)
            here = pl.ds(at, QUERY_TILE)
            scores = dot(keys, query_cols[:, here])
            if allowed is not None:
                scores = jnp.where(allowed, scores, masked_score)
            weights = jnp.exp(scores)
            score_grad = (weights * dot(values, grad_cols[:, here])).astype(bf16)
            pair_total[...] += dot(score_grad, query_rows[here]) + dot(
                weights.astype(bf16), grad_rows[here]
            )
            query_total[:, here] += dot(key_cols[block], score_grad)
            return nothing

        tile(block // 2, 0, places_allowed(scalars, block & 1))
        lax.fori_loop(block // 2 + 1, TILES, tile, 0)
        out[block, 0:BLOCK_ROWS] = pair_total[...].astype(bf16)
        return nothing

    lax.fori_loop(0, BLOCKS, key_block, 0)
    for block in range(BLOCKS):
        here = slice(block * TOKENS, (block + 1) * TOKENS)
        out[block, BLOCK_ROWS:] = fold_rows(
            transposed(query_total[:, here] * 0.125).astype(bf16)
        )


def feed_kernel(
    scalars,
    x0,
    x1,
    x2,
    x3,
    a0,
    a1,
    a2,
    a3,
    c0,
    c1,
    c2,
    c3,
    weights,
    params,
    bias,
    residual_out,
    own_attended,
    normed_out,
    hidden_out,
    pre_grad_out,
    output_part,
    normed_part,
    sums,
):
    member = scalars[0]
    residual = jnp.concatenate([x0[...], x1[...], x2[...], x3[...]], axis=0).astype(f32)
    residual = residual + params[4:5]
    select_row = lax.broadcasted_iota(jnp.int32, (GROUP_WIDTH, GROUP_WIDTH), 0)
    select_col = lax.broadcasted_iota(jnp.int32, (GROUP_WIDTH, GROUP_WIDTH), 1)
    wanted = (select_col // 6) * 24 + member * 6 + select_col % 6
    own = jnp.zeros((BLOCK_ROWS, GROUP_WIDTH), f32)
    for group, arrived in enumerate((a0, a1, a2, a3)):
        slots = []
        for slot in range(QUARTERS):
            quarter = (slot - group) % QUARTERS
            slots.append(
                jnp.concatenate(
                    [unfold_rows(arrived[head * QUARTERS + quarter]) for head in range(GROUP_HEADS)],
                    axis=1,
                )
            )
        attended = jnp.concatenate(slots, axis=0)
        first = ((member - group + GROUPS) & (GROUPS - 1)) * GROUP_WIDTH
        rows = pl.ds(pl.multiple_of(first, 64), GROUP_WIDTH)
        residual = residual + dot(attended, weights[rows, WIDTH : 2 * WIDTH])
        chosen = jnp.where(select_row + first == wanted, 1.0, 0.0).astype(bf16)
        own = own + dot(attended, chosen)
    own_attended[...] = own.astype(bf16)
    residual_out[...] = residual[0:TOKENS]
    unit, _ = unit_norm(residual)
    normed = (unit * params[5:6] + params[6:7]).astype(bf16)
    normed_out[...] = normed
    pre = dot(normed, weights[:, 0:WIDTH]) + bias[...]
    slope = 0.7978845608028654
    tanh = jnp.tanh(slope * (pre + 0.044715 * pre * pre * pre))
    hidden = (0.5 * pre * (1.0 + tanh)).astype(bf16)
    hidden_out[...] = hidden
    output_part[...] = dot(hidden, weights[:, 2 * WIDTH :]).astype(bf16)
    cotangent = jnp.concatenate([c0[...], c1[...], c2[...], c3[...]], axis=0)
    hidden_grad = dot(cotangent, weights[:, 2 * WIDTH :], 1, 1)
    pull = 0.5 * (1.0 + tanh) + 0.5 * pre * (1.0 - tanh * tanh) * slope * (
        1.0 + 3.0 * 0.044715 * pre * pre
    )
    pre_grad = (hidden_grad * pull).astype(bf16)
    pre_grad_out[...] = pre_grad
    normed_grad = dot(pre_grad, weights[:, 0:WIDTH], 1, 1)
    normed_part[...] = normed_grad.astype(bf16)
    sums[0:1] = jnp.sum(normed_grad * unit, axis=0, keepdims=True)
    sums[1:2] = jnp.sum(normed_grad, axis=0, keepdims=True)
    sums[2:3] = jnp.sum(pre_grad.astype(f32), axis=0, keepdims=True)
    sums[3:8] = jnp.zeros((5, WIDTH), f32)


def residual_kernel(residual, p0, p1, p2, p3, cotangent, params, grad_out, branch_out, sums):
    normed_grad = (p0[...].astype(f32) + p1[...].astype(f32)) + (
        p2[...].astype(f32) + p3[...].astype(f32)
    )
    unit, inverse = unit_norm(residual[...])
    grad_rows = cotangent[...].astype(f32)
    residual_grad = grad_rows + norm_backward(normed_grad, unit, inverse, params[5:6])
    grad_out[...] = residual_grad
    branch_grad = residual_grad.astype(bf16)
    branch_out[...] = branch_grad
    sums[0:1] = jnp.sum(branch_grad.astype(f32), axis=0, keepdims=True)
    sums[1:2] = jnp.sum(grad_rows, axis=0, keepdims=True)
    sums[2:8] = jnp.zeros((6, WIDTH), f32)


def branch_kernel(scalars, b0, b1, b2, b3, weights, out):
    branch_grad = jnp.concatenate([b0[...], b1[...], b2[...], b3[...]], axis=0)
    first = scalars[0] * GROUP_WIDTH
    rows = pl.ds(pl.multiple_of(first, 64), GROUP_WIDTH)
    attended_grad = dot(branch_grad, weights[rows, WIDTH : 2 * WIDTH], 1, 1).astype(bf16)
    for head in range(GROUP_HEADS):
        for quarter in range(QUARTERS):
            out[head * QUARTERS + quarter] = fold_rows(
                attended_grad[
                    quarter * TOKENS : (quarter + 1) * TOKENS,
                    head * HEAD_DIM : (head + 1) * HEAD_DIM,
                ]
            )
    out[GROUP_HEADS * QUARTERS :] = jnp.zeros((BLOCKS - GROUP_HEADS * QUARTERS, 64, 128), bf16)


def weight_grad_kernel(
    hidden, c0, c1, c2, c3, normed, pre_grad, own_attended, b0, b1, b2, b3, out
):
    cotangent = jnp.concatenate([c0[...], c1[...], c2[...], c3[...]], axis=0)
    branch_grad = jnp.concatenate([b0[...], b1[...], b2[...], b3[...]], axis=0)
    down = dot(hidden[...], cotangent, 0, 0).reshape(32, 24, WIDTH)
    out[:, 0:24] = down.astype(out.dtype)
    up = dot(normed[...], pre_grad[...], 0, 0).reshape(32, 24, WIDTH)
    out[:, 24:48] = up.astype(out.dtype)
    attn = dot(own_attended[...], branch_grad, 0, 0).reshape(32, 6, WIDTH)
    out[:, 48:54] = attn.astype(out.dtype)
    out[:, 54:56] = jnp.zeros((32, 2, WIDTH), out.dtype)


def mixed_back_kernel(arrived, x0, x1, x2, x3, params, weight, normed_part, weight_grad, sums, mixed_sums):
    rows = jnp.concatenate([x0[...], x1[...], x2[...], x3[...]], axis=0).astype(f32)
    unit, _ = unit_norm(rows)
    normed = (unit * params[0:1] + params[1:2]).astype(bf16)
    pieces, queries = [], []
    for head in range(GROUP_HEADS):
        pair = jnp.zeros((BLOCK_ROWS, 128), f32)
        for quarter in range(QUARTERS):
            pair = pair + arrived[head * QUARTERS + quarter, 0:BLOCK_ROWS].astype(f32)
        pieces.append(pair.astype(bf16))
        queries.append(
            jnp.concatenate(
                [
                    unfold_rows(arrived[head * QUARTERS + quarter, BLOCK_ROWS:])
                    for quarter in range(QUARTERS)
                ],
                axis=0,
            )
        )
    mixed_grad = jnp.concatenate(pieces + queries, axis=1)
    normed_grad = dot(mixed_grad, weight[...], 1, 1)
    normed_part[...] = normed_grad.astype(bf16)
    weight_grad[...] = dot(normed, mixed_grad, 0, 0).astype(bf16)
    sums[0:1] = jnp.sum(normed_grad * unit, axis=0, keepdims=True)
    sums[1:2] = jnp.sum(normed_grad, axis=0, keepdims=True)
    sums[2:8] = jnp.zeros((6, WIDTH), f32)
    mixed_sums[0:1] = jnp.sum(mixed_grad.astype(f32), axis=0, keepdims=True)
    mixed_sums[1:8] = jnp.zeros((7, 3 * GROUP_WIDTH), f32)


def adam_step(weight, gradient, first, second, rate, decay_flag):
    moment = first_decay * first + (1.0 - first_decay) * gradient
    squares = second_decay * second + (1.0 - second_decay) * gradient * gradient
    fix_one = 1.0 - first_decay**STEP
    fix_two = 1.0 - second_decay**STEP
    direction = moment / fix_one / (jnp.sqrt(squares / fix_two) + adam_epsilon)
    updated = weight - rate * (direction + decay_flag * weight_decay * weight)
    return (updated, moment, squares)


def per_device(
    inputs,
    cotangent,
    qkv_weight,
    attn_weight,
    up_weight,
    down_weight,
    vectors,
    qkv_first,
    attn_first,
    up_first,
    down_first,
    vector_first,
    qkv_second,
    attn_second,
    up_second,
    down_second,
    vector_second,
):
    member = lax.axis_index("heads")
    scalars = jnp.stack([member, lax.axis_index("blk") % QUARTERS]).astype(jnp.int32)

    with jax.named_scope("parameter_copies"):
        by_head = qkv_weight.astype(bf16).reshape(6, 3, GROUPS, GROUP_HEADS, HEAD_DIM)
        pairs = by_head[:, 1:].transpose(2, 0, 3, 1, 4).reshape(GROUPS, 6, 384)
        alone = by_head[:, 0].transpose(1, 0, 2, 3).reshape(GROUPS, 6, GROUP_WIDTH)
        leaving = jnp.concatenate([pairs, alone], axis=2).reshape(GROUPS, 27, 128)
        vector_row = jnp.pad(vectors.astype(bf16).reshape(1, 1, 72), ((0, 0), (0, 0), (0, 56)))
        leaving = jnp.concatenate(
            [leaving, jnp.broadcast_to(vector_row, (GROUPS, 1, 128))], axis=1
        )
        leaving = jnp.broadcast_to(leaving[None], (32, GROUPS, 28, 128)).reshape(OWNERS, 28, 128)
        came = lax.all_to_all(leaving, EVERY, 0, 0, tiled=True)
        qkv_copy = came[:, :27].reshape(WIDTH, 576)
        params = came[:, 27, :72].reshape(OWNERS, 12, 6).transpose(1, 0, 2).reshape(12, WIDTH)
        params = params.astype(f32)

        up_parts = up_weight.astype(bf16).reshape(6, 32, GROUPS, 24).transpose(2, 0, 1, 3)
        up_parts = up_parts.reshape(GROUPS, 6, WIDTH)
        attn_parts = jnp.broadcast_to(attn_weight.astype(bf16)[None], (GROUPS, 6, WIDTH))
        leaving = jnp.concatenate([up_parts, attn_parts], axis=2)
        came = lax.all_to_all(leaving, "heads", 0, 0, tiled=True).reshape(24, 2 * WIDTH)
        rest = jnp.concatenate([came, down_weight.astype(bf16)], axis=1)
        rest_copy = lax.all_gather(rest, ("dp", "blk"), axis=0, tiled=True)

    params_rows = jnp.concatenate([params, jnp.zeros((4, WIDTH), f32)], axis=0)
    query_bias = lax.dynamic_slice_in_dim(params[2], member * GROUP_WIDTH, GROUP_WIDTH)
    value_bias = lax.dynamic_slice_in_dim(params[3], member * GROUP_WIDTH, GROUP_WIDTH)
    pair_bias = jnp.stack(
        [jnp.zeros((GROUP_HEADS, HEAD_DIM), f32), value_bias.reshape(GROUP_HEADS, HEAD_DIM)], axis=1
    ).reshape(-1)
    mixed_bias = jnp.concatenate([pair_bias, query_bias])[None]
    hidden_bias = lax.dynamic_slice_in_dim(params[8:12].reshape(32, GROUPS, 24), member, 1, 1)
    hidden_bias = hidden_bias.reshape(1, WIDTH)

    x_slots = gather_slots(inputs)
    c_slots = gather_slots(cotangent)
    (leaving,) = call(project_kernel, [((BLOCKS, 576, 128), bf16)], inputs=7)(
        *x_slots, params_rows, qkv_copy, mixed_bias
    )
    arrived = lax.all_to_all(leaving, "blk", 0, 0, tiled=True)
    attended, attended_cols, log_total = call(
        attend_kernel,
        [
            ((BLOCKS, 64, 128), bf16),
            ((HEAD_DIM, QUERY_ROWS), f32),
            ((1, QUERY_ROWS), f32),
        ],
        scratch=[
            pltpu.VMEM((HEAD_DIM, QUERY_ROWS), bf16),
            pltpu.VMEM((BLOCKS, 80, BLOCK_ROWS), bf16),
        ],
        smem=1,
        inputs=1,
    )(scalars, arrived)
    attended = lax.all_to_all(attended, "blk", 0, 0, tiled=True)
    a_slots = gather_slots(attended)
    (
        residual,
        own_attended,
        normed_two,
        hidden,
        pre_grad,
        output_part,
        normed_part,
        feed_sums,
    ) = call(
        feed_kernel,
        [
            ((TOKENS, WIDTH), f32),
            ((BLOCK_ROWS, GROUP_WIDTH), bf16),
            ((BLOCK_ROWS, WIDTH), bf16),
            ((BLOCK_ROWS, WIDTH), bf16),
            ((BLOCK_ROWS, WIDTH), bf16),
            ((BLOCK_ROWS, WIDTH), bf16),
            ((BLOCK_ROWS, WIDTH), bf16),
            ((8, WIDTH), f32),
        ],
        smem=1,
        inputs=15,
    )(scalars, *x_slots, *a_slots, *c_slots, rest_copy, params_rows, hidden_bias)

    def slots_of(array):
        return [array[slot * TOKENS : (slot + 1) * TOKENS] for slot in range(GROUPS)]

    normed_slots = return_slots(slots_of(normed_part))
    output_slots = return_slots(slots_of(output_part))
    residual_grad, branch_grad, residual_sums = call(
        residual_kernel,
        [((TOKENS, WIDTH), f32), ((TOKENS, WIDTH), bf16), ((8, WIDTH), f32)],
        inputs=7,
    )(residual, *normed_slots, cotangent, params_rows)
    b_slots = gather_slots(branch_grad)
    (leaving,) = call(branch_kernel, [((BLOCKS, 64, 128), bf16)], smem=1, inputs=5)(
        scalars, *b_slots, rest_copy
    )
    out_grads = lax.all_to_all(leaving, "blk", 0, 0, tiled=True)
    (rest_grad,) = call(weight_grad_kernel, [((32, 56, WIDTH), f32)], inputs=12)(
        hidden, *c_slots, normed_two, pre_grad, own_attended, *b_slots
    )
    rest_sum = lax.psum_scatter(
        rest_grad.reshape(32 * 56, WIDTH), ("dp", "blk"), scatter_dimension=0, tiled=True
    )
    (leaving,) = call(
        attend_back_kernel,
        [((BLOCKS, 576, 128), bf16)],
        scratch=[
            pltpu.VMEM((128, QUERY_ROWS), bf16),
            pltpu.VMEM((128, QUERY_ROWS), bf16),
            pltpu.VMEM((QUERY_ROWS, 128), bf16),
            pltpu.VMEM((QUERY_ROWS, 128), bf16),
            pltpu.VMEM((BLOCKS, HEAD_DIM, BLOCK_ROWS), bf16),
            pltpu.VMEM((HEAD_DIM, QUERY_ROWS), f32),
            pltpu.VMEM((BLOCK_ROWS, 128), f32),
        ],
        smem=1,
        inputs=4,
    )(scalars, arrived, out_grads, attended_cols, log_total)
    mixed_parts = lax.all_to_all(leaving, "blk", 0, 0, tiled=True)
    normed_one_part, qkv_grad, mixed_rows, mixed_sums = call(
        mixed_back_kernel,
        [
            ((BLOCK_ROWS, WIDTH), bf16),
            ((WIDTH, 576), bf16),
            ((8, WIDTH), f32),
            ((8, 576), f32),
        ],
        inputs=7,
    )(mixed_parts, *x_slots, params_rows, qkv_copy)
    normed_slots = return_slots(slots_of(normed_one_part))

    with jax.named_scope("vector_terms"):
        pair_sums = mixed_sums[0, :384].reshape(GROUP_HEADS, 2, HEAD_DIM)[:, 1].reshape(1, -1)
        at_group = (lax.iota(jnp.int32, GROUPS) == member).astype(f32)[:, None]
        query_row = (at_group * mixed_sums[0:1, 384:]).reshape(1, WIDTH)
        value_row = (at_group * pair_sums).reshape(1, WIDTH)
        hidden_rows = (at_group[None] * feed_sums[2].reshape(32, 1, 24)).reshape(4, WIDTH)
        vector_grad = jnp.concatenate(
            [
                mixed_rows[0:2],
                query_row,
                value_row,
                residual_sums[0:1],
                feed_sums[0:2],
                residual_sums[1:2],
                hidden_rows,
            ],
            axis=0,
        )
        vector_grad = vector_grad.reshape(12, OWNERS, 6).transpose(1, 0, 2).reshape(OWNERS, 72)
        vector_high = vector_grad.astype(bf16)
        vector_low = (vector_grad - vector_high.astype(f32)).astype(bf16)
        vector_pair = jnp.pad(
            jnp.stack([vector_high, vector_low], axis=1), ((0, 0), (0, 0), (0, 56))
        )
        leaving = jnp.concatenate([qkv_grad.reshape(OWNERS, 27, 128), vector_pair], axis=1)
        came = lax.all_to_all(leaving, EVERY, 0, 0, tiled=True)
        vector_sum = jnp.sum(came[:, 27:, :72].astype(f32), axis=(0, 1)).reshape(12, 6)
        qkv_sum = jnp.sum(came[:, :27].reshape(32, GROUPS, 27, 128).astype(f32), axis=0)
        qkv_sum = qkv_sum.reshape(GROUPS, 6, 576)
        pairs = qkv_sum[:, :, :384].reshape(GROUPS, 6, GROUP_HEADS, 2, HEAD_DIM)
        pairs = pairs.transpose(1, 3, 0, 2, 4).reshape(6, 2 * WIDTH)
        alone = qkv_sum[:, :, 384:].transpose(1, 0, 2).reshape(6, WIDTH)
        qkv_sum = jnp.concatenate([alone, pairs], axis=1)

    down_sum = rest_sum[0:24]
    attn_sum = rest_sum[48:54]
    up_sum = lax.all_to_all(
        rest_sum[24:48].reshape(GROUPS, 6, WIDTH), "heads", 0, 0, tiled=True
    )
    up_sum = up_sum.reshape(GROUPS, 6, 32, 24).transpose(1, 2, 0, 3).reshape(6, HIDDEN)

    def summed(slots):
        slots = [slot.astype(f32) for slot in slots]
        return (slots[0] + slots[1]) + (slots[2] + slots[3])

    output = (residual + summed(output_slots) + params[7]).astype(bf16)
    unit, inverse = unit_norm(inputs.astype(f32))
    input_grad = residual_grad + norm_backward(summed(normed_slots), unit, inverse, params[0])

    qkv_updated, qkv_moment, qkv_squares = adam_step(
        qkv_weight, qkv_sum, qkv_first, qkv_second, 0.04, 1.0
    )
    attn_updated, attn_moment, attn_squares = adam_step(
        attn_weight, attn_sum, attn_first, attn_second, 0.1, 1.0
    )
    up_updated, up_moment, up_squares = adam_step(up_weight, up_sum, up_first, up_second, 0.03, 1.0)
    down_updated, down_moment, down_squares = adam_step(
        down_weight, down_sum, down_first, down_second, 0.02, 1.0
    )
    vector_updated, vector_moment, vector_squares = adam_step(
        vectors, vector_sum, vector_first, vector_second, 0.7, 0.0
    )
    return (
        output,
        input_grad,
        qkv_updated,
        attn_updated,
        up_updated,
        down_updated,
        vector_updated,
        qkv_moment,
        attn_moment,
        up_moment,
        down_moment,
        vector_moment,
        qkv_squares,
        attn_squares,
        up_squares,
        down_squares,
        vector_squares,
    )


def solution(mesh):
    rows, columns = P(EVERY, None), P(None, EVERY)
    weights = (rows, rows, rows, rows, columns)
    return jax.shard_map(
        per_device,
        mesh=mesh,
        in_specs=(rows, rows) + weights * 3,
        out_specs=(rows, rows) + weights * 3,
        check_vma=False,
    )
```

```python
import functools

import jax
import jax.numpy as jnp
from jax import lax
from jax.experimental import pallas as pl
from jax.experimental.pallas import tpu as pltpu
from jax.sharding import PartitionSpec as P

STEP = 10
WIDTH = 768
HIDDEN = 3072
HEAD_DIM = 64
GROUPS = 4
GROUP_HEADS = 3
GROUP_WIDTH = 192
BLOCKS = 16
QUARTERS = 4
TOKENS = 128
BLOCK_ROWS = 512
OWNERS = 128
QUERY_TILE = 256
QUERY_ROWS = BLOCKS * TOKENS
TILES = QUERY_ROWS // QUERY_TILE
EVERY = ("dp", "blk", "heads")

norm_epsilon = 1e-05
first_decay = 0.9
second_decay = 0.95
adam_epsilon = 1e-08
weight_decay = 0.1
masked_score = -1e30
bf16 = jnp.bfloat16
f32 = jnp.float32


def shifted(array, axis, by):
    count = lax.axis_size(axis)
    return lax.ppermute(array, axis, [(i, (i + by) % count) for i in range(count)])


def gather_slots(array):
    return [array] + [shifted(array, "heads", by) for by in range(1, GROUPS)]


def return_slots(slots):
    return [slots[0]] + [shifted(slots[by], "heads", -by) for by in range(1, GROUPS)]


def exchange_groups(parts):
    member = lax.axis_index("heads")
    rolled = lax.dynamic_slice_in_dim(jnp.concatenate([parts, parts]), member, GROUPS, 0)
    got = [rolled[0]] + [shifted(rolled[by], "heads", by) for by in range(1, GROUPS)]
    turned = jnp.stack(got[::-1])
    return lax.dynamic_slice_in_dim(
        jnp.concatenate([turned, turned]), GROUPS - 1 - member, GROUPS, 0
    )


def dot(left, right, left_dim=1, right_dim=0):
    return lax.dot_general(
        left, right, (((left_dim,), (right_dim,)), ((), ())), preferred_element_type=f32
    )


def unit_norm(values):
    centred = values - jnp.mean(values, axis=-1, keepdims=True)
    variance = jnp.mean(centred * centred, axis=-1, keepdims=True)
    inverse = lax.rsqrt(variance + norm_epsilon)
    return centred * inverse, inverse


def norm_backward(grad_rows, unit_rows, inverse, gain):
    scaled = grad_rows * gain
    mean_grad = jnp.mean(scaled, axis=-1, keepdims=True)
    mean_unit = jnp.mean(scaled * unit_rows, axis=-1, keepdims=True)
    return inverse * (scaled - mean_grad - unit_rows * mean_unit)


def call(kernel, outs, scratch=(), smem=0, inputs=0, micros=5):
    in_specs = [pl.BlockSpec(memory_space=pltpu.SMEM)] * smem + [
        pl.BlockSpec(memory_space=pltpu.VMEM)
    ] * inputs
    return pl.pallas_call(
        kernel,
        out_shape=[jax.ShapeDtypeStruct(shape, dtype) for shape, dtype in outs],
        in_specs=in_specs,
        out_specs=[pl.BlockSpec(memory_space=pltpu.VMEM)] * len(outs),
        scratch_shapes=list(scratch),
        compiler_params=pltpu.CompilerParams(vmem_limit_bytes=56 * 2**20),
        cost_estimate=pl.CostEstimate(
            flops=micros * 10**9, bytes_accessed=2**20, transcendentals=0
        ),
    )


def fold_rows(rows):
    return jnp.concatenate([rows[:64], rows[64:]], axis=1)


def unfold_rows(folded):
    return jnp.concatenate([folded[:, :64], folded[:, 64:]], axis=0)


def project_kernel(scalars, x0, x1, x2, x3, weight, out, params):
    params[...] = transposed(weight[:, 576:640])[0:16]
    rows = jnp.concatenate([x0[...], x1[...], x2[...], x3[...]], axis=0).astype(f32)
    unit, _ = unit_norm(rows)
    normed = (unit * params[0:1] + params[1:2]).astype(bf16)
    own = jnp.zeros((2, GROUP_WIDTH), f32)
    for group in range(GROUPS):
        part = params[2:4, group * GROUP_WIDTH : (group + 1) * GROUP_WIDTH]
        own = own + jnp.where(scalars[0] == group, part, 0.0)
    pieces = []
    for head in range(GROUP_HEADS):
        pieces.append(jnp.zeros((1, HEAD_DIM), f32))
        pieces.append(own[1:2, head * HEAD_DIM : (head + 1) * HEAD_DIM])
    bias = jnp.concatenate(pieces + [own[0:1]], axis=1)
    mixed = (dot(normed, weight[:, 0:576]) + bias).astype(bf16)
    for head in range(GROUP_HEADS):
        pair = mixed[:, head * 128 : (head + 1) * 128]
        first = 384 + head * HEAD_DIM
        queries = mixed[:, first : first + HEAD_DIM]
        for quarter in range(QUARTERS):
            place = head * QUARTERS + quarter
            out[place, 0:BLOCK_ROWS] = pair
            out[place, BLOCK_ROWS:] = fold_rows(queries[quarter * TOKENS : (quarter + 1) * TOKENS])
    out[GROUP_HEADS * QUARTERS :] = jnp.zeros((BLOCKS - GROUP_HEADS * QUARTERS, 576, 128), bf16)


def place_bias(scalars, offset):
    member, quarter = scalars[0], scalars[1]
    key_row = lax.broadcasted_iota(jnp.int32, (BLOCK_ROWS, QUERY_TILE), 0)
    query_row = lax.broadcasted_iota(jnp.int32, (BLOCK_ROWS, QUERY_TILE), 1)
    key_sub = (member - key_row // TOKENS + GROUPS) & (GROUPS - 1)
    key_place = offset * BLOCK_ROWS + key_sub * TOKENS + (key_row & (TOKENS - 1))
    query_sub = (member - quarter + GROUPS) & (GROUPS - 1)
    query_place = (
        (query_row // TOKENS) * BLOCK_ROWS + query_sub * TOKENS + (query_row & (TOKENS - 1))
    )
    return jnp.where(key_place <= query_place, 0.0, masked_score)


def transposed(values):
    return jnp.transpose(values.astype(f32), (1, 0))


def attend_kernel(scalars, arrived, out, out_cols, log_total, query_cols, value_cols, bias):
    for offset in range(2):
        bias[offset] = place_bias(scalars, offset)
    for block in range(BLOCKS):
        queries = unfold_rows(arrived[block, BLOCK_ROWS:])
        query_cols[:, block * TOKENS : (block + 1) * TOKENS] = (
            transposed(queries) * 0.125
        ).astype(bf16)
        value_cols[block, 0:64] = transposed(arrived[block, 0:BLOCK_ROWS])[64:128].astype(bf16)
        value_cols[block, 64:80] = jnp.ones((16, BLOCK_ROWS), bf16)

    def visit(block, carried, queries, offset=None):
        peak, total = carried
        scores = dot(arrived[block, 0:BLOCK_ROWS, 0:64], queries)
        if offset is not None:
            scores = scores + bias[offset]
        new_peak = jnp.maximum(peak, jnp.max(scores, axis=0, keepdims=True))
        weights = jnp.exp(scores - new_peak).astype(bf16)
        total = total * jnp.exp(peak - new_peak) + dot(value_cols[block], weights)
        return new_peak, total

    def finish(block, at, carried):
        peak, total = carried
        row_total = total[64:65]
        attended = total[0:64] / row_total
        out_cols[:, pl.ds(at, QUERY_TILE)] = attended
        log_total[:, pl.ds(at, QUERY_TILE)] = peak + jnp.log(row_total)
        attended_rows = transposed(attended).astype(bf16)
        out[block] = fold_rows(attended_rows[0:TOKENS])
        out[block + 1] = fold_rows(attended_rows[TOKENS:])

    def tiles(step, nothing):
        at = pl.multiple_of(step * 2 * QUERY_TILE, 2 * QUERY_TILE)
        after = pl.multiple_of(at + QUERY_TILE, QUERY_TILE)
        early = query_cols[:, pl.ds(at, QUERY_TILE)]
        late = query_cols[:, pl.ds(after, QUERY_TILE)]
        start = (
            jnp.full((1, QUERY_TILE), masked_score, f32),
            jnp.zeros((80, QUERY_TILE), f32),
        )
        first = 4 * step
        early_sums, late_sums = start, start
        for offset in range(2):
            early_sums = visit(first + offset, early_sums, early, offset)
            late_sums = visit(first + offset, late_sums, late)
        for offset in range(2):
            late_sums = visit(first + 2 + offset, late_sums, late, offset)

        def both(turn, carried):
            early_sums, late_sums = carried
            for block in (2 * turn, 2 * turn + 1):
                early_sums = visit(block, early_sums, early)
                late_sums = visit(block, late_sums, late)
            return early_sums, late_sums

        early_sums, late_sums = lax.fori_loop(0, 2 * step, both, (early_sums, late_sums))
        finish(first, at, early_sums)
        finish(first + 2, after, late_sums)
        return nothing

    lax.fori_loop(0, TILES // 2, tiles, 0)


def split_three(values):
    high = values.astype(bf16)
    rest = values - high.astype(f32)
    middle = rest.astype(bf16)
    low = (rest - middle.astype(f32)).astype(bf16)
    return high, middle, low


def attend_back_kernel(
    scalars,
    arrived,
    grads,
    out_cols,
    log_total,
    out,
    query_cols,
    grad_cols,
    query_rows,
    grad_rows,
    key_cols,
    query_total,
    pair_total,
    bias,
):
    for offset in range(2):
        bias[offset] = place_bias(scalars, offset)
    key_lane = lax.broadcasted_iota(jnp.int32, (BLOCK_ROWS, 128), 1)
    zeros = jnp.zeros((TOKENS, 64), bf16)
    lane_row = lax.broadcasted_iota(jnp.int32, (64, TOKENS), 0)
    for block in range(BLOCKS):
        here = slice(block * TOKENS, (block + 1) * TOKENS)
        queries = unfold_rows(arrived[block, BLOCK_ROWS:]) * 0.125
        query_rows[here] = jnp.concatenate([queries, zeros], axis=1)
        query_cols[0:64, here] = transposed(queries).astype(bf16)
        parts = split_three(-log_total[:, here])
        query_cols[64:128, here] = jnp.where(
            lane_row == 0,
            parts[0].astype(f32),
            jnp.where(
                lane_row == 1,
                parts[1].astype(f32),
                jnp.where(lane_row == 2, parts[2].astype(f32), 0.0),
            ),
        ).astype(bf16)
        out_grad = unfold_rows(grads[block])
        grad_rows[here] = jnp.concatenate([zeros, out_grad], axis=1)
        grad_col = transposed(out_grad)
        grad_cols[64:128, here] = grad_col.astype(bf16)
        delta = jnp.sum(grad_col * out_cols[:, here], axis=0, keepdims=True)
        parts = split_three(-delta)
        grad_cols[0:64, here] = jnp.where(
            lane_row == 0,
            parts[0].astype(f32),
            jnp.where(
                lane_row == 1,
                parts[1].astype(f32),
                jnp.where(lane_row == 2, parts[2].astype(f32), 0.0),
            ),
        ).astype(bf16)
        key_cols[block] = transposed(arrived[block, 0:BLOCK_ROWS])[0:64].astype(bf16)
    query_total[...] = jnp.zeros((64, QUERY_ROWS), f32)

    def key_block(block, nothing):
        pair = arrived[block, 0:BLOCK_ROWS]
        keys = jnp.where(key_lane < 64, pair, jnp.where(key_lane < 67, 1.0, 0.0).astype(bf16))
        values = jnp.where(key_lane >= 64, pair, jnp.where(key_lane < 3, 1.0, 0.0).astype(bf16))
        pair_total[...] = jnp.zeros((BLOCK_ROWS, 128), f32)

        def tile(at, offset=None):
            here = pl.ds(at, QUERY_TILE)
            scores = dot(keys, query_cols[:, here])
            if offset is not None:
                scores = scores + bias[offset]
            weights = jnp.exp(scores)
            score_grad = (weights * dot(values, grad_cols[:, here])).astype(bf16)
            query_total[:, here] += dot(key_cols[block], score_grad)
            return dot(score_grad, query_rows[here]) + dot(weights.astype(bf16), grad_rows[here])

        def places(step):
            at = pl.multiple_of(step * 2 * QUERY_TILE, 2 * QUERY_TILE)
            return at, pl.multiple_of(at + QUERY_TILE, QUERY_TILE)

        step = block // 4
        offset = block & 1
        early, late = places(step)

        @pl.when(block % 4 < 2)
        def _():
            pair_total[...] += tile(early, offset) + tile(late)

        @pl.when(block % 4 >= 2)
        def _():
            pair_total[...] += tile(late, offset)

        def both(step, nothing):
            early, late = places(step)
            pair_total[...] += tile(early) + tile(late)
            return nothing

        lax.fori_loop(step + 1, TILES // 2, both, 0)
        out[block, 0:BLOCK_ROWS] = pair_total[...].astype(bf16)
        return nothing

    lax.fori_loop(0, BLOCKS, key_block, 0)
    for block in range(BLOCKS):
        here = slice(block * TOKENS, (block + 1) * TOKENS)
        out[block, BLOCK_ROWS:] = fold_rows(
            transposed(query_total[:, here] * 0.125).astype(bf16)
        )


def feed_kernel(
    scalars,
    x0,
    x1,
    x2,
    x3,
    a0,
    a1,
    a2,
    a3,
    c0,
    c1,
    c2,
    c3,
    weights,
    params,
    bias,
    residual_out,
    own_attended,
    normed_out,
    hidden_out,
    pre_grad_out,
    output_part,
    normed_part,
    sums,
):
    member = scalars[0]
    residual = jnp.concatenate([x0[...], x1[...], x2[...], x3[...]], axis=0).astype(f32)
    residual = residual + params[4:5]
    select_row = lax.broadcasted_iota(jnp.int32, (GROUP_WIDTH, GROUP_WIDTH), 0)
    select_col = lax.broadcasted_iota(jnp.int32, (GROUP_WIDTH, GROUP_WIDTH), 1)
    wanted = (select_col // 6) * 24 + member * 6 + select_col % 6
    own = jnp.zeros((BLOCK_ROWS, GROUP_WIDTH), f32)
    for group, arrived in enumerate((a0, a1, a2, a3)):
        slots = []
        for slot in range(QUARTERS):
            quarter = (slot - group) % QUARTERS
            slots.append(
                jnp.concatenate(
                    [unfold_rows(arrived[head * QUARTERS + quarter]) for head in range(GROUP_HEADS)],
                    axis=1,
                )
            )
        attended = jnp.concatenate(slots, axis=0)
        first = ((member - group + GROUPS) & (GROUPS - 1)) * GROUP_WIDTH
        rows = pl.ds(pl.multiple_of(first, 64), GROUP_WIDTH)
        residual = residual + dot(attended, weights[rows, WIDTH : 2 * WIDTH])
        chosen = jnp.where(select_row + first == wanted, 1.0, 0.0).astype(bf16)
        own = own + dot(attended, chosen)
    own_attended[...] = own.astype(bf16)
    residual_out[...] = residual[0:TOKENS]
    unit, _ = unit_norm(residual)
    normed = (unit * params[5:6] + params[6:7]).astype(bf16)
    normed_out[...] = normed
    pre = dot(normed, weights[:, 0:WIDTH]) + bias[...]
    slope = 0.7978845608028654
    tanh = jnp.tanh(slope * (pre + 0.044715 * pre * pre * pre))
    hidden = (0.5 * pre * (1.0 + tanh)).astype(bf16)
    hidden_out[...] = hidden
    output_part[...] = dot(hidden, weights[:, 2 * WIDTH :]).astype(bf16)
    cotangent = jnp.concatenate([c0[...], c1[...], c2[...], c3[...]], axis=0)
    hidden_grad = dot(cotangent, weights[:, 2 * WIDTH :], 1, 1)
    pull = 0.5 * (1.0 + tanh) + 0.5 * pre * (1.0 - tanh * tanh) * slope * (
        1.0 + 3.0 * 0.044715 * pre * pre
    )
    pre_grad = (hidden_grad * pull).astype(bf16)
    pre_grad_out[...] = pre_grad
    normed_grad = dot(pre_grad, weights[:, 0:WIDTH], 1, 1)
    normed_part[...] = normed_grad.astype(bf16)
    sums[0:1] = jnp.sum(normed_grad * unit, axis=0, keepdims=True)
    sums[1:2] = jnp.sum(normed_grad, axis=0, keepdims=True)
    sums[2:3] = jnp.sum(pre_grad.astype(f32), axis=0, keepdims=True)
    sums[3:8] = jnp.zeros((5, WIDTH), f32)


def residual_kernel(
    scalars,
    residual,
    p0,
    p1,
    p2,
    p3,
    cotangent,
    params,
    attn_weight,
    grad_out,
    branch_out,
    sums,
    d0,
    d1,
    d2,
    d3,
):
    normed_grad = (p0[...].astype(f32) + p1[...].astype(f32)) + (
        p2[...].astype(f32) + p3[...].astype(f32)
    )
    unit, inverse = unit_norm(residual[...])
    grad_rows = cotangent[...].astype(f32)
    residual_grad = grad_rows + norm_backward(normed_grad, unit, inverse, params[5:6])
    grad_out[...] = residual_grad
    branch_grad = residual_grad.astype(bf16)
    branch_out[...] = branch_grad
    sums[0:1] = jnp.sum(branch_grad.astype(f32), axis=0, keepdims=True)
    sums[1:2] = jnp.sum(grad_rows, axis=0, keepdims=True)
    sums[2:8] = jnp.zeros((6, WIDTH), f32)
    for group, out in enumerate((d0, d1, d2, d3)):
        first = ((scalars[0] + group) & (GROUPS - 1)) * GROUP_WIDTH
        rows = pl.ds(pl.multiple_of(first, 64), GROUP_WIDTH)
        attended_grad = dot(branch_grad, attn_weight[rows], 1, 1).astype(bf16)
        for head in range(GROUP_HEADS):
            out[head] = fold_rows(attended_grad[:, head * HEAD_DIM : (head + 1) * HEAD_DIM])


def weight_grad_kernel(
    hidden, c0, c1, c2, c3, normed, pre_grad, own_attended, b0, b1, b2, b3, out
):
    cotangent = jnp.concatenate([c0[...], c1[...], c2[...], c3[...]], axis=0)
    branch_grad = jnp.concatenate([b0[...], b1[...], b2[...], b3[...]], axis=0)
    down = dot(hidden[...], cotangent, 0, 0).reshape(32, 24, WIDTH)
    up = dot(normed[...], pre_grad[...], 0, 0).reshape(32, 24, WIDTH)
    attn = dot(own_attended[...], branch_grad, 0, 0).reshape(32, 6, WIDTH)
    rows = jnp.concatenate([down, up, attn, jnp.zeros((32, 2, WIDTH), f32)], axis=1)
    out[...] = rows.astype(bf16)


def mixed_back_kernel(
    scalars,
    arrived,
    x0,
    x1,
    x2,
    x3,
    params,
    weight,
    early_terms,
    normed_part,
    weight_grad,
    vector_terms,
):
    rows = jnp.concatenate([x0[...], x1[...], x2[...], x3[...]], axis=0).astype(f32)
    unit, _ = unit_norm(rows)
    normed = (unit * params[0:1] + params[1:2]).astype(bf16)
    pieces, queries = [], []
    for head in range(GROUP_HEADS):
        pair = jnp.zeros((BLOCK_ROWS, 128), f32)
        for quarter in range(QUARTERS):
            pair = pair + arrived[head * QUARTERS + quarter, 0:BLOCK_ROWS].astype(f32)
        pieces.append(pair.astype(bf16))
        queries.append(
            jnp.concatenate(
                [
                    unfold_rows(arrived[head * QUARTERS + quarter, BLOCK_ROWS:])
                    for quarter in range(QUARTERS)
                ],
                axis=0,
            )
        )
    mixed_grad = jnp.concatenate(pieces + queries, axis=1)
    normed_grad = dot(mixed_grad, weight[:, 0:576], 1, 1)
    normed_part[...] = normed_grad.astype(bf16)
    column_sums = jnp.sum(mixed_grad.astype(f32), axis=0, keepdims=True)
    value_sums = jnp.concatenate(
        [column_sums[:, head * 128 + 64 : head * 128 + 128] for head in range(GROUP_HEADS)], axis=1
    )
    lane = lax.broadcasted_iota(jnp.int32, (1, WIDTH), 1)
    first = scalars[0] * GROUP_WIDTH
    own = (lane >= first) & (lane < first + GROUP_WIDTH)
    vector_terms[...] = early_terms[...]
    vector_terms[0:1] = jnp.sum(normed_grad * unit, axis=0, keepdims=True)
    vector_terms[1:2] = jnp.sum(normed_grad, axis=0, keepdims=True)
    vector_terms[2:3] = jnp.where(own, jnp.concatenate([column_sums[:, 384:]] * GROUPS, axis=1), 0.0)
    vector_terms[3:4] = jnp.where(own, jnp.concatenate([value_sums] * GROUPS, axis=1), 0.0)
    high = vector_terms[...].astype(bf16).astype(f32)
    low = vector_terms[...] - high
    columns = transposed(jnp.concatenate([high, low, jnp.zeros((32, WIDTH), f32)], axis=0))
    weight_grad[...] = jnp.concatenate([dot(normed, mixed_grad, 0, 0), columns], axis=1).astype(bf16)


def adam_step(weight, gradient, first, second, rate, decay_flag):
    moment = first_decay * first + (1.0 - first_decay) * gradient
    squares = second_decay * second + (1.0 - second_decay) * gradient * gradient
    fix_one = 1.0 - first_decay**STEP
    fix_two = 1.0 - second_decay**STEP
    direction = moment / fix_one / (jnp.sqrt(squares / fix_two) + adam_epsilon)
    updated = weight - rate * (direction + decay_flag * weight_decay * weight)
    return (updated, moment, squares)


def per_device(
    inputs,
    cotangent,
    qkv_weight,
    attn_weight,
    up_weight,
    down_weight,
    vectors,
    qkv_first,
    attn_first,
    up_first,
    down_first,
    vector_first,
    qkv_second,
    attn_second,
    up_second,
    down_second,
    vector_second,
):
    member = lax.axis_index("heads")
    scalars = jnp.stack([member, lax.axis_index("blk") % QUARTERS]).astype(jnp.int32)

    with jax.named_scope("qkv_copies"):
        by_head = qkv_weight.astype(bf16).reshape(6, 3, GROUPS, GROUP_HEADS, HEAD_DIM)
        pairs = by_head[:, 1:].transpose(2, 0, 3, 1, 4).reshape(GROUPS, 6, 384)
        alone = by_head[:, 0].transpose(1, 0, 2, 3).reshape(GROUPS, 6, GROUP_WIDTH)
        vector_cols = jnp.broadcast_to(vectors.astype(bf16).T[None], (GROUPS, 6, 12))
        leaving = jnp.concatenate(
            [pairs, alone, vector_cols, jnp.zeros((GROUPS, 6, 52), bf16)], axis=2
        ).reshape(GROUPS, 30, 128)
        leaving = jnp.broadcast_to(leaving[None], (32, GROUPS, 30, 128)).reshape(OWNERS, 30, 128)
        leaving, later_inputs, later_up, later_attn = lax.optimization_barrier(
            (leaving, inputs, up_weight, attn_weight)
        )
        came = lax.all_to_all(leaving, EVERY, 0, 0, tiled=True)
        qkv_copy = came.reshape(WIDTH, 640)
        x_slots = gather_slots(later_inputs)
    leaving, params_rows = call(
        project_kernel, [((BLOCKS, 576, 128), bf16), ((16, WIDTH), f32)], smem=1, inputs=5
    )(scalars, *x_slots, qkv_copy)

    leaving, later_cotangent = lax.optimization_barrier((leaving, cotangent))
    arrived = lax.all_to_all(leaving, "blk", 0, 0, tiled=True)
    with jax.named_scope("other_copies"):
        up_parts = later_up.astype(bf16).reshape(6, 32, GROUPS, 24).transpose(2, 0, 1, 3)
        up_parts = up_parts.reshape(GROUPS, 6, WIDTH)
        attn_parts = jnp.broadcast_to(later_attn.astype(bf16)[None], (GROUPS, 6, WIDTH))
        sent = jnp.concatenate([up_parts, attn_parts], axis=2)
        came = exchange_groups(sent).reshape(24, 2 * WIDTH)
        rest = jnp.concatenate([came, down_weight.astype(bf16)], axis=1)
        rest_copy = lax.all_gather(rest, ("dp", "blk"), axis=0, tiled=True)
    attn_copy = rest_copy[:, WIDTH : 2 * WIDTH]
    c_slots = gather_slots(later_cotangent)
    arrived, c_slots = lax.optimization_barrier((arrived, c_slots))
    hidden_bias = lax.dynamic_slice_in_dim(
        params_rows[8:12].reshape(32, GROUPS, 24), member, 1, 1
    )
    hidden_bias = hidden_bias.reshape(1, WIDTH)

    attended, attended_cols, log_total = call(
        attend_kernel,
        [
            ((BLOCKS, 64, 128), bf16),
            ((HEAD_DIM, QUERY_ROWS), f32),
            ((1, QUERY_ROWS), f32),
        ],
        scratch=[
            pltpu.VMEM((HEAD_DIM, QUERY_ROWS), bf16),
            pltpu.VMEM((BLOCKS, 80, BLOCK_ROWS), bf16),
            pltpu.VMEM((2, BLOCK_ROWS, QUERY_TILE), f32),
        ],
        smem=1,
        inputs=1,
        micros=36,
    )(scalars, arrived)
    attended = lax.all_to_all(attended, "blk", 0, 0, tiled=True)
    a_slots = gather_slots(attended[: GROUP_HEADS * QUARTERS])
    (
        residual,
        own_attended,
        normed_two,
        hidden,
        pre_grad,
        output_part,
        normed_part,
        feed_sums,
    ) = call(
        feed_kernel,
        [
            ((TOKENS, WIDTH), f32),
            ((BLOCK_ROWS, GROUP_WIDTH), bf16),
            ((BLOCK_ROWS, WIDTH), bf16),
            ((BLOCK_ROWS, WIDTH), bf16),
            ((BLOCK_ROWS, WIDTH), bf16),
            ((BLOCK_ROWS, WIDTH), bf16),
            ((BLOCK_ROWS, WIDTH), bf16),
            ((8, WIDTH), f32),
        ],
        smem=1,
        inputs=15,
        micros=8,
    )(scalars, *x_slots, *a_slots, *c_slots, rest_copy, params_rows, hidden_bias)

    def slots_of(array):
        return [array[slot * TOKENS : (slot + 1) * TOKENS] for slot in range(GROUPS)]

    normed_slots = return_slots(slots_of(normed_part))
    residual_grad, branch_grad, residual_sums, *grad_slots = call(
        residual_kernel,
        [((TOKENS, WIDTH), f32), ((TOKENS, WIDTH), bf16), ((8, WIDTH), f32)]
        + [((GROUP_HEADS, 64, 128), bf16)] * GROUPS,
        smem=1,
        inputs=8,
        micros=3,
    )(scalars, residual, *normed_slots, cotangent, params_rows, attn_copy)
    grad_slots = grad_slots[:1] + [
        shifted(grad_slots[by], "heads", by) for by in range(1, GROUPS)
    ]
    leaving = jnp.stack(grad_slots, axis=1).reshape(GROUP_HEADS * QUARTERS, 64, 128)
    leaving = jnp.concatenate([leaving, jnp.zeros((4, 64, 128), bf16)], axis=0)
    leaving, later_output, later_branch = lax.optimization_barrier(
        (leaving, output_part, branch_grad)
    )
    out_grads = lax.all_to_all(leaving, "blk", 0, 0, tiled=True)
    b_slots = gather_slots(later_branch)
    (rest_grad,) = call(weight_grad_kernel, [((32, 56, WIDTH), bf16)], inputs=12, micros=6)(
        hidden, *c_slots, normed_two, pre_grad, own_attended, *b_slots
    )
    rest_grad, out_grads = lax.optimization_barrier((rest_grad, out_grads))
    rest_parts = lax.all_to_all(rest_grad, ("dp", "blk"), 0, 0, tiled=True)
    (leaving,) = call(
        attend_back_kernel,
        [((BLOCKS, 576, 128), bf16)],
        scratch=[
            pltpu.VMEM((128, QUERY_ROWS), bf16),
            pltpu.VMEM((128, QUERY_ROWS), bf16),
            pltpu.VMEM((QUERY_ROWS, 128), bf16),
            pltpu.VMEM((QUERY_ROWS, 128), bf16),
            pltpu.VMEM((BLOCKS, HEAD_DIM, BLOCK_ROWS), bf16),
            pltpu.VMEM((HEAD_DIM, QUERY_ROWS), f32),
            pltpu.VMEM((BLOCK_ROWS, 128), f32),
            pltpu.VMEM((2, BLOCK_ROWS, QUERY_TILE), f32),
        ],
        smem=1,
        inputs=4,
        micros=35,
    )(scalars, arrived, out_grads, attended_cols, log_total)
    leaving, rest_parts, later_output = lax.optimization_barrier(
        (leaving, rest_parts, later_output)
    )
    mixed_parts = lax.all_to_all(leaving, "blk", 0, 0, tiled=True)
    output_slots = return_slots(slots_of(later_output))
    rest_sum = jnp.sum(rest_parts.astype(f32), axis=0)
    down_sum = rest_sum[0:24]
    attn_sum = rest_sum[48:54]
    up_sum = exchange_groups(rest_sum[24:48].reshape(GROUPS, 6, WIDTH))
    up_sum = up_sum.reshape(GROUPS, 6, 32, 24).transpose(1, 2, 0, 3).reshape(6, HIDDEN)

    at_group = (lax.iota(jnp.int32, GROUPS) == member).astype(f32)[:, None]
    early_terms = jnp.concatenate(
        [
            jnp.zeros((4, WIDTH), f32),
            residual_sums[0:1],
            feed_sums[0:2],
            residual_sums[1:2],
            (at_group[None] * feed_sums[2].reshape(32, 1, 24)).reshape(4, WIDTH),
            jnp.zeros((4, WIDTH), f32),
        ],
        axis=0,
    )
    normed_one_part, qkv_grad = call(
        mixed_back_kernel,
        [((BLOCK_ROWS, WIDTH), bf16), ((WIDTH, 640), bf16)],
        scratch=[pltpu.VMEM((16, WIDTH), f32)],
        smem=1,
        inputs=8,
    )(scalars, mixed_parts, *x_slots, params_rows, qkv_copy, early_terms)
    with jax.named_scope("qkv_terms"):
        came = lax.all_to_all(qkv_grad.reshape(OWNERS, 30, 128), EVERY, 0, 0, tiled=True)
        qkv_sum = jnp.sum(came.reshape(32, GROUPS, 30, 128).astype(f32), axis=0)
        qkv_sum = qkv_sum.reshape(GROUPS, 6, 640)
        vector_sum = jnp.sum(qkv_sum[:, :, 576:608], axis=0)
        vector_sum = (vector_sum[:, 0:12] + vector_sum[:, 16:28]).T
        pairs = qkv_sum[:, :, :384].reshape(GROUPS, 6, GROUP_HEADS, 2, HEAD_DIM)
        pairs = pairs.transpose(1, 3, 0, 2, 4).reshape(6, 2 * WIDTH)
        alone = qkv_sum[:, :, 384:576].transpose(1, 0, 2).reshape(6, WIDTH)
        qkv_sum = jnp.concatenate([alone, pairs], axis=1)
    normed_slots = return_slots(slots_of(normed_one_part))

    def summed(slots):
        slots = [slot.astype(f32) for slot in slots]
        return (slots[0] + slots[1]) + (slots[2] + slots[3])

    output = (residual + summed(output_slots) + params_rows[7]).astype(bf16)
    unit, inverse = unit_norm(inputs.astype(f32))
    input_grad = residual_grad + norm_backward(summed(normed_slots), unit, inverse, params_rows[0])

    qkv_updated, qkv_moment, qkv_squares = adam_step(
        qkv_weight, qkv_sum, qkv_first, qkv_second, 0.04, 1.0
    )
    attn_updated, attn_moment, attn_squares = adam_step(
        attn_weight, attn_sum, attn_first, attn_second, 0.1, 1.0
    )
    up_updated, up_moment, up_squares = adam_step(up_weight, up_sum, up_first, up_second, 0.03, 1.0)
    down_updated, down_moment, down_squares = adam_step(
        down_weight, down_sum, down_first, down_second, 0.02, 1.0
    )
    vector_updated, vector_moment, vector_squares = adam_step(
        vectors, vector_sum, vector_first, vector_second, 0.7, 0.0
    )
    return (
        output,
        input_grad,
        qkv_updated,
        attn_updated,
        up_updated,
        down_updated,
        vector_updated,
        qkv_moment,
        attn_moment,
        up_moment,
        down_moment,
        vector_moment,
        qkv_squares,
        attn_squares,
        up_squares,
        down_squares,
        vector_squares,
    )


def solution(mesh):
    rows, columns = P(EVERY, None), P(None, EVERY)
    weights = (rows, rows, rows, rows, columns)
    return jax.shard_map(
        per_device,
        mesh=mesh,
        in_specs=(rows, rows) + weights * 3,
        out_specs=(rows, rows) + weights * 3,
        check_vma=False,
    )
```

```python
import functools

import jax
import jax.numpy as jnp
from jax import lax
from jax.experimental import pallas as pl
from jax.experimental.pallas import tpu as pltpu
from jax.sharding import PartitionSpec as P

STEP = 10
WIDTH = 768
HIDDEN = 3072
HEAD_DIM = 64
GROUPS = 4
GROUP_HEADS = 3
GROUP_WIDTH = 192
BLOCKS = 16
QUARTERS = 4
TOKENS = 128
BLOCK_ROWS = 512
OWNERS = 128
QUERY_ROWS = BLOCKS * TOKENS
EVERY = ("dp", "blk", "heads")

norm_epsilon = 1e-05
first_decay = 0.9
second_decay = 0.95
adam_epsilon = 1e-08
weight_decay = 0.1
masked_score = -1e30
bf16 = jnp.bfloat16
f32 = jnp.float32


def shifted(array, axis, by):
    count = lax.axis_size(axis)
    return lax.ppermute(array, axis, [(i, (i + by) % count) for i in range(count)])


def gather_slots(array):
    return [array] + [shifted(array, "heads", by) for by in range(1, GROUPS)]


def return_slots(slots):
    return [slots[0]] + [shifted(slots[by], "heads", -by) for by in range(1, GROUPS)]


def exchange_groups(parts):
    member = lax.axis_index("heads")
    rolled = lax.dynamic_slice_in_dim(jnp.concatenate([parts, parts]), member, GROUPS, 0)
    got = [rolled[0]] + [shifted(rolled[by], "heads", by) for by in range(1, GROUPS)]
    turned = jnp.stack(got[::-1])
    return lax.dynamic_slice_in_dim(
        jnp.concatenate([turned, turned]), GROUPS - 1 - member, GROUPS, 0
    )


def dot(left, right, left_dim=1, right_dim=0):
    return lax.dot_general(
        left, right, (((left_dim,), (right_dim,)), ((), ())), preferred_element_type=f32
    )


def unit_norm(values):
    centred = values - jnp.mean(values, axis=-1, keepdims=True)
    variance = jnp.mean(centred * centred, axis=-1, keepdims=True)
    inverse = lax.rsqrt(variance + norm_epsilon)
    return centred * inverse, inverse


def norm_backward(grad_rows, unit_rows, inverse, gain):
    scaled = grad_rows * gain
    mean_grad = jnp.mean(scaled, axis=-1, keepdims=True)
    mean_unit = jnp.mean(scaled * unit_rows, axis=-1, keepdims=True)
    return inverse * (scaled - mean_grad - unit_rows * mean_unit)


def call(kernel, outs, scratch=(), smem=0, inputs=0, outside=0, micros=5):
    in_specs = [pl.BlockSpec(memory_space=pltpu.SMEM)] * smem + [
        pl.BlockSpec(memory_space=pltpu.VMEM)
    ] * inputs
    in_specs = in_specs + [pl.BlockSpec(memory_space=pl.ANY)] * outside
    return pl.pallas_call(
        kernel,
        out_shape=[jax.ShapeDtypeStruct(shape, dtype) for shape, dtype in outs],
        in_specs=in_specs,
        out_specs=[pl.BlockSpec(memory_space=pltpu.VMEM)] * len(outs),
        scratch_shapes=list(scratch),
        compiler_params=pltpu.CompilerParams(vmem_limit_bytes=56 * 2**20),
        cost_estimate=pl.CostEstimate(
            flops=micros * 10**9, bytes_accessed=2**20, transcendentals=0
        ),
    )


def fold_rows(rows):
    return jnp.concatenate([rows[:64], rows[64:]], axis=1)


def unfold_rows(folded):
    return jnp.concatenate([folded[:, :64], folded[:, 64:]], axis=0)


def project_kernel(scalars, x0, x1, x2, x3, weight, out, params):
    params[...] = transposed(weight[:, 576:640])[0:16]
    rows = jnp.concatenate([x0[...], x1[...], x2[...], x3[...]], axis=0).astype(f32)
    unit, _ = unit_norm(rows)
    normed = (unit * params[0:1] + params[1:2]).astype(bf16)
    own = jnp.zeros((2, GROUP_WIDTH), f32)
    for group in range(GROUPS):
        part = params[2:4, group * GROUP_WIDTH : (group + 1) * GROUP_WIDTH]
        own = own + jnp.where(scalars[0] == group, part, 0.0)
    pieces = []
    for head in range(GROUP_HEADS):
        pieces.append(jnp.zeros((1, HEAD_DIM), f32))
        pieces.append(own[1:2, head * HEAD_DIM : (head + 1) * HEAD_DIM])
    bias = jnp.concatenate(pieces + [own[0:1]], axis=1)
    mixed = (dot(normed, weight[:, 0:576]) + bias).astype(bf16)
    for head in range(GROUP_HEADS):
        pair = mixed[:, head * 128 : (head + 1) * 128]
        first = 384 + head * HEAD_DIM
        queries = mixed[:, first : first + HEAD_DIM]
        for quarter in range(QUARTERS):
            place = head * QUARTERS + quarter
            out[place, 0:BLOCK_ROWS] = pair
            out[place, BLOCK_ROWS:] = fold_rows(queries[quarter * TOKENS : (quarter + 1) * TOKENS])
    out[GROUP_HEADS * QUARTERS :] = jnp.zeros((BLOCKS - GROUP_HEADS * QUARTERS, 576, 128), bf16)


def place_gap(scalars):
    member, quarter = scalars[0], scalars[1]
    key_row = lax.broadcasted_iota(jnp.int32, (BLOCK_ROWS, TOKENS), 0)
    query_row = lax.broadcasted_iota(jnp.int32, (BLOCK_ROWS, TOKENS), 1)
    key_sub = (member - key_row // TOKENS + GROUPS) & (GROUPS - 1)
    query_sub = (member - quarter + GROUPS) & (GROUPS - 1)
    return (query_sub - key_sub) * TOKENS + query_row - (key_row & (TOKENS - 1))


def mask_lead(scores, allowed):
    masked = jnp.where(allowed, scores[:, :TOKENS], masked_score)
    if scores.shape[1] == TOKENS:
        return masked
    return jnp.concatenate([masked, scores[:, TOKENS:]], axis=1)


def transposed(values):
    return jnp.transpose(values.astype(f32), (1, 0))


def attend_kernel(
    scalars, arrived, out, out_cols, log_total, query_cols, value_cols, gap, peak, total
):
    gap[...] = place_gap(scalars).astype(f32)
    for block in range(BLOCKS):
        queries = unfold_rows(arrived[block, BLOCK_ROWS:])
        query_cols[:, block * TOKENS : (block + 1) * TOKENS] = (
            transposed(queries) * 0.125
        ).astype(bf16)
        value_cols[block, 0:64] = transposed(arrived[block, 0:BLOCK_ROWS])[64:128].astype(bf16)
        value_cols[block, 64:80] = jnp.ones((16, BLOCK_ROWS), bf16)
    peak[...] = jnp.full((1, QUERY_ROWS), masked_score, f32)
    total[...] = jnp.zeros((80, QUERY_ROWS), f32)
    for block in range(BLOCKS):
        first = block * TOKENS
        scores = dot(arrived[block, 0:BLOCK_ROWS, 0:64], query_cols[:, first:])
        scores = mask_lead(scores, gap[...] >= 0.0)
        old = peak[:, first:]
        new = jnp.maximum(old, jnp.max(scores, axis=0, keepdims=True))
        weights = jnp.exp(scores - new).astype(bf16)
        total[:, first:] = total[:, first:] * jnp.exp(old - new) + dot(value_cols[block], weights)
        peak[:, first:] = new
    row_total = total[64:65]
    out_cols[...] = total[0:64] / row_total
    log_total[...] = peak[...] + jnp.log(row_total)
    for block in range(BLOCKS):
        attended = out_cols[:, block * TOKENS : (block + 1) * TOKENS]
        out[block] = fold_rows(transposed(attended).astype(bf16))


def split_three(values):
    high = values.astype(bf16)
    rest = values - high.astype(f32)
    middle = rest.astype(bf16)
    low = (rest - middle.astype(f32)).astype(bf16)
    return high, middle, low


def attend_back_kernel(
    scalars,
    arrived,
    grads,
    out_cols,
    log_total,
    out,
    query_cols,
    grad_cols,
    query_rows,
    grad_rows,
    key_cols,
    query_total,
    gap,
):
    gap[...] = place_gap(scalars).astype(f32)
    key_lane = lax.broadcasted_iota(jnp.int32, (BLOCK_ROWS, 128), 1)
    lane_row = lax.broadcasted_iota(jnp.int32, (64, TOKENS), 0)
    zeros = jnp.zeros((TOKENS, 64), bf16)

    def part_rows(values):
        parts = [part.astype(f32) for part in split_three(values)]
        rows = jnp.where(lane_row == 2, parts[2], 0.0)
        rows = jnp.where(lane_row == 1, parts[1], rows)
        return jnp.where(lane_row == 0, parts[0], rows).astype(bf16)

    for block in range(BLOCKS):
        here = slice(block * TOKENS, (block + 1) * TOKENS)
        queries = unfold_rows(arrived[block, BLOCK_ROWS:]) * 0.125
        query_rows[here] = jnp.concatenate([queries, zeros], axis=1)
        query_cols[0:64, here] = transposed(queries).astype(bf16)
        query_cols[64:128, here] = part_rows(-log_total[:, here])
        out_grad = unfold_rows(grads[block])
        grad_rows[here] = jnp.concatenate([zeros, out_grad], axis=1)
        grad_col = transposed(out_grad)
        grad_cols[64:128, here] = grad_col.astype(bf16)
        delta = jnp.sum(grad_col * out_cols[:, here], axis=0, keepdims=True)
        grad_cols[0:64, here] = part_rows(-delta)
        key_cols[block] = transposed(arrived[block, 0:BLOCK_ROWS])[0:64].astype(bf16)
    query_total[...] = jnp.zeros((64, QUERY_ROWS), f32)
    for block in range(BLOCKS):
        first = block * TOKENS
        pair = arrived[block, 0:BLOCK_ROWS]
        keys = jnp.where(key_lane < 64, pair, jnp.where(key_lane < 67, 1.0, 0.0).astype(bf16))
        values = jnp.where(key_lane >= 64, pair, jnp.where(key_lane < 3, 1.0, 0.0).astype(bf16))
        scores = dot(keys, query_cols[:, first:])
        weights = jnp.exp(mask_lead(scores, gap[...] >= 0.0))
        score_grad = (weights * dot(values, grad_cols[:, first:])).astype(bf16)
        out[block, 0:BLOCK_ROWS] = (
            dot(score_grad, query_rows[first:]) + dot(weights.astype(bf16), grad_rows[first:])
        ).astype(bf16)
        query_total[:, first:] += dot(key_cols[block], score_grad)
    for block in range(BLOCKS):
        here = slice(block * TOKENS, (block + 1) * TOKENS)
        out[block, BLOCK_ROWS:] = fold_rows(
            transposed(query_total[:, here] * 0.125).astype(bf16)
        )


def store_slots(outs, values):
    for slot, out in enumerate(outs):
        out[...] = values[slot * TOKENS : (slot + 1) * TOKENS]


def feed_kernel(
    scalars,
    x0,
    x1,
    x2,
    x3,
    a0,
    a1,
    a2,
    a3,
    c0,
    c1,
    c2,
    c3,
    weights,
    params,
    bias,
    residual_out,
    own_attended,
    kept,
    sent,
    sums,
    *parts,
):
    *parts, both = parts
    output_parts, normed_parts = parts[:GROUPS], parts[GROUPS:]
    member = scalars[0]
    residual = jnp.concatenate([x0[...], x1[...], x2[...], x3[...]], axis=0).astype(f32)
    residual = residual + params[4:5]
    select_row = lax.broadcasted_iota(jnp.int32, (GROUP_WIDTH, GROUP_WIDTH), 0)
    select_col = lax.broadcasted_iota(jnp.int32, (GROUP_WIDTH, GROUP_WIDTH), 1)
    wanted = (select_col // 6) * 24 + member * 6 + select_col % 6
    own = jnp.zeros((BLOCK_ROWS, GROUP_WIDTH), f32)
    for group, arrived in enumerate((a0, a1, a2, a3)):
        slots = []
        for slot in range(QUARTERS):
            quarter = (slot - group) % QUARTERS
            slots.append(
                jnp.concatenate(
                    [unfold_rows(arrived[head * QUARTERS + quarter]) for head in range(GROUP_HEADS)],
                    axis=1,
                )
            )
        attended = jnp.concatenate(slots, axis=0)
        first = ((member - group + GROUPS) & (GROUPS - 1)) * GROUP_WIDTH
        rows = pl.ds(pl.multiple_of(first, 64), GROUP_WIDTH)
        residual = residual + dot(attended, weights[rows, WIDTH : 2 * WIDTH])
        chosen = jnp.where(select_row + first == wanted, 1.0, 0.0).astype(bf16)
        own = own + dot(attended, chosen)
    own_attended[...] = own.astype(bf16)
    residual_out[...] = residual[0:TOKENS]
    unit, _ = unit_norm(residual)
    normed = (unit * params[5:6] + params[6:7]).astype(bf16)
    pre = dot(normed, weights[:, 0:WIDTH]) + bias[...]
    slope = 0.7978845608028654
    tanh = jnp.tanh(slope * (pre + 0.044715 * pre * pre * pre))
    hidden = (0.5 * pre * (1.0 + tanh)).astype(bf16)
    store_slots(output_parts, dot(hidden, weights[:, 2 * WIDTH :]).astype(bf16))
    cotangent = jnp.concatenate([c0[...], c1[...], c2[...], c3[...]], axis=0)
    hidden_grad = dot(cotangent, weights[:, 2 * WIDTH :], 1, 1)
    pull = 0.5 * (1.0 + tanh) + 0.5 * pre * (1.0 - tanh * tanh) * slope * (
        1.0 + 3.0 * 0.044715 * pre * pre
    )
    pre_grad = (hidden_grad * pull).astype(bf16)
    down = dot(hidden, cotangent, 0, 0).reshape(32, 24, WIDTH)
    up = dot(normed, pre_grad, 0, 0).reshape(32, 24, WIDTH)
    both[...] = jnp.concatenate([down, up], axis=1).astype(bf16)
    core = scalars[2]
    kept[...] = both[pl.ds(core * BLOCKS, BLOCKS)]
    sent[...] = both[pl.ds((1 - core) * BLOCKS, BLOCKS)]
    normed_grad = dot(pre_grad, weights[:, 0:WIDTH], 1, 1)
    store_slots(normed_parts, normed_grad.astype(bf16))
    sums[0:1] = jnp.sum(normed_grad * unit, axis=0, keepdims=True)
    sums[1:2] = jnp.sum(normed_grad, axis=0, keepdims=True)
    sums[2:3] = jnp.sum(pre_grad.astype(f32), axis=0, keepdims=True)
    sums[3:8] = jnp.zeros((5, WIDTH), f32)


def residual_kernel(
    scalars,
    residual,
    p0,
    p1,
    p2,
    p3,
    cotangent,
    params,
    weights,
    grad_out,
    branch_out,
    sums,
    d0,
    d1,
    d2,
    d3,
    attn_weight,
    copied,
):
    copy = pltpu.make_async_copy(weights.at[:, pl.ds(WIDTH, WIDTH)], attn_weight, copied)
    copy.start()
    normed_grad = (p0[...].astype(f32) + p1[...].astype(f32)) + (
        p2[...].astype(f32) + p3[...].astype(f32)
    )
    unit, inverse = unit_norm(residual[...])
    grad_rows = cotangent[...].astype(f32)
    residual_grad = grad_rows + norm_backward(normed_grad, unit, inverse, params[5:6])
    grad_out[...] = residual_grad
    branch_grad = residual_grad.astype(bf16)
    branch_out[...] = branch_grad
    sums[0:1] = jnp.sum(branch_grad.astype(f32), axis=0, keepdims=True)
    sums[1:2] = jnp.sum(grad_rows, axis=0, keepdims=True)
    sums[2:8] = jnp.zeros((6, WIDTH), f32)
    copy.wait()
    for group, out in enumerate((d0, d1, d2, d3)):
        first = ((scalars[0] + group) & (GROUPS - 1)) * GROUP_WIDTH
        rows = pl.ds(pl.multiple_of(first, 64), GROUP_WIDTH)
        attended_grad = dot(branch_grad, attn_weight[rows], 1, 1).astype(bf16)
        for head in range(GROUP_HEADS):
            out[head] = fold_rows(attended_grad[:, head * HEAD_DIM : (head + 1) * HEAD_DIM])


def rest_grad_kernel(kept, came, own_attended, b0, b1, b2, b3, out):
    branch_grad = jnp.concatenate([b0[...], b1[...], b2[...], b3[...]], axis=0)
    attn = dot(own_attended[...], branch_grad, 0, 0).reshape(2, BLOCKS, 6, WIDTH)
    feed = kept[...].astype(f32) + came[...].astype(f32)
    empty = jnp.zeros((BLOCKS, 4, WIDTH), f32)
    out[...] = jnp.concatenate([feed, attn[0], attn[1], empty], axis=1).astype(bf16)


def mixed_back_kernel(
    scalars,
    arrived,
    x0,
    x1,
    x2,
    x3,
    params,
    weight,
    early_terms,
    weight_grad,
    p0,
    p1,
    p2,
    p3,
    vector_terms,
):
    rows = jnp.concatenate([x0[...], x1[...], x2[...], x3[...]], axis=0).astype(f32)
    unit, _ = unit_norm(rows)
    normed = (unit * params[0:1] + params[1:2]).astype(bf16)
    pieces, queries = [], []
    for head in range(GROUP_HEADS):
        pair = jnp.zeros((BLOCK_ROWS, 128), f32)
        for quarter in range(QUARTERS):
            pair = pair + arrived[head * QUARTERS + quarter, 0:BLOCK_ROWS].astype(f32)
        pieces.append(pair.astype(bf16))
        queries.append(
            jnp.concatenate(
                [
                    unfold_rows(arrived[head * QUARTERS + quarter, BLOCK_ROWS:])
                    for quarter in range(QUARTERS)
                ],
                axis=0,
            )
        )
    mixed_grad = jnp.concatenate(pieces + queries, axis=1)
    normed_grad = dot(mixed_grad, weight[:, 0:576], 1, 1)
    store_slots((p0, p1, p2, p3), normed_grad.astype(bf16))
    column_sums = jnp.sum(mixed_grad.astype(f32), axis=0, keepdims=True)
    value_sums = jnp.concatenate(
        [column_sums[:, head * 128 + 64 : head * 128 + 128] for head in range(GROUP_HEADS)], axis=1
    )
    lane = lax.broadcasted_iota(jnp.int32, (1, WIDTH), 1)
    first = scalars[0] * GROUP_WIDTH
    own = (lane >= first) & (lane < first + GROUP_WIDTH)
    vector_terms[...] = early_terms[...]
    vector_terms[0:1] = jnp.sum(normed_grad * unit, axis=0, keepdims=True)
    vector_terms[1:2] = jnp.sum(normed_grad, axis=0, keepdims=True)
    vector_terms[2:3] = jnp.where(own, jnp.concatenate([column_sums[:, 384:]] * GROUPS, axis=1), 0.0)
    vector_terms[3:4] = jnp.where(own, jnp.concatenate([value_sums] * GROUPS, axis=1), 0.0)
    high = vector_terms[...].astype(bf16).astype(f32)
    low = vector_terms[...] - high
    columns = transposed(jnp.concatenate([high, low, jnp.zeros((32, WIDTH), f32)], axis=0))
    weight_grad[...] = jnp.concatenate([dot(normed, mixed_grad, 0, 0), columns], axis=1).astype(bf16)


def adam_step(weight, gradient, first, second, rate, decay_flag):
    moment = first_decay * first + (1.0 - first_decay) * gradient
    squares = second_decay * second + (1.0 - second_decay) * gradient * gradient
    fix_one = 1.0 - first_decay**STEP
    fix_two = 1.0 - second_decay**STEP
    direction = moment / fix_one / (jnp.sqrt(squares / fix_two) + adam_epsilon)
    updated = weight - rate * (direction + decay_flag * weight_decay * weight)
    return (updated, moment, squares)


def per_device(
    inputs,
    cotangent,
    qkv_weight,
    attn_weight,
    up_weight,
    down_weight,
    vectors,
    qkv_first,
    attn_first,
    up_first,
    down_first,
    vector_first,
    qkv_second,
    attn_second,
    up_second,
    down_second,
    vector_second,
):
    member = lax.axis_index("heads")
    scalars = jnp.stack(
        [member, lax.axis_index("blk") % QUARTERS, lax.axis_index("dp")]
    ).astype(jnp.int32)

    with jax.named_scope("qkv_copies"):
        by_head = qkv_weight.astype(bf16).reshape(6, 3, GROUPS, GROUP_HEADS, HEAD_DIM)
        pairs = by_head[:, 1:].transpose(2, 0, 3, 1, 4).reshape(GROUPS, 6, 384)
        alone = by_head[:, 0].transpose(1, 0, 2, 3).reshape(GROUPS, 6, GROUP_WIDTH)
        vector_cols = jnp.broadcast_to(vectors.astype(bf16).T[None], (GROUPS, 6, 12))
        leaving = jnp.concatenate(
            [pairs, alone, vector_cols, jnp.zeros((GROUPS, 6, 52), bf16)], axis=2
        ).reshape(GROUPS, 30, 128)
        leaving = jnp.broadcast_to(leaving[None], (32, GROUPS, 30, 128)).reshape(OWNERS, 30, 128)
        leaving, later_inputs, later_up, later_attn = lax.optimization_barrier(
            (leaving, inputs, up_weight, attn_weight)
        )
        came = lax.all_to_all(leaving, EVERY, 0, 0, tiled=True)
        qkv_copy = came.reshape(WIDTH, 640)
        x_slots = gather_slots(later_inputs)
    leaving, params_rows = call(
        project_kernel, [((BLOCKS, 576, 128), bf16), ((16, WIDTH), f32)], smem=1, inputs=5
    )(scalars, *x_slots, qkv_copy)

    leaving, later_cotangent = lax.optimization_barrier((leaving, cotangent))
    arrived = lax.all_to_all(leaving, "blk", 0, 0, tiled=True)
    with jax.named_scope("other_copies"):
        up_parts = later_up.astype(bf16).reshape(6, 32, GROUPS, 24).transpose(2, 0, 1, 3)
        up_parts = up_parts.reshape(GROUPS, 6, WIDTH)
        attn_parts = jnp.broadcast_to(later_attn.astype(bf16)[None], (GROUPS, 6, WIDTH))
        sent = jnp.concatenate([up_parts, attn_parts], axis=2)
        came = exchange_groups(sent).reshape(24, 2 * WIDTH)
        rest = jnp.concatenate([came, down_weight.astype(bf16)], axis=1)
        rest_copy = lax.all_gather(rest, ("dp", "blk"), axis=0, tiled=True)
    c_slots = gather_slots(later_cotangent)
    arrived, c_slots = lax.optimization_barrier((arrived, c_slots))
    hidden_bias = lax.dynamic_slice_in_dim(
        params_rows[8:12].reshape(32, GROUPS, 24), member, 1, 1
    )
    hidden_bias = hidden_bias.reshape(1, WIDTH)

    attended, attended_cols, log_total = call(
        attend_kernel,
        [
            ((BLOCKS, 64, 128), bf16),
            ((HEAD_DIM, QUERY_ROWS), f32),
            ((1, QUERY_ROWS), f32),
        ],
        scratch=[
            pltpu.VMEM((HEAD_DIM, QUERY_ROWS), bf16),
            pltpu.VMEM((BLOCKS, 80, BLOCK_ROWS), bf16),
            pltpu.VMEM((BLOCK_ROWS, TOKENS), f32),
            pltpu.VMEM((1, QUERY_ROWS), f32),
            pltpu.VMEM((80, QUERY_ROWS), f32),
        ],
        smem=1,
        inputs=1,
        micros=50,
    )(scalars, arrived)
    attended = lax.all_to_all(attended, "blk", 0, 0, tiled=True)
    a_slots = gather_slots(attended[: GROUP_HEADS * QUARTERS])
    (
        residual,
        own_attended,
        kept,
        sent,
        feed_sums,
        *feed_parts,
    ) = call(
        feed_kernel,
        [
            ((TOKENS, WIDTH), f32),
            ((BLOCK_ROWS, GROUP_WIDTH), bf16),
            ((BLOCKS, 48, WIDTH), bf16),
            ((BLOCKS, 48, WIDTH), bf16),
            ((8, WIDTH), f32),
        ]
        + [((TOKENS, WIDTH), bf16)] * (2 * GROUPS),
        smem=1,
        inputs=15,
        scratch=[pltpu.VMEM((2 * BLOCKS, 48, WIDTH), bf16)],
        micros=10,
    )(scalars, *x_slots, *a_slots, *c_slots, rest_copy, params_rows, hidden_bias)

    output_parts, normed_parts = feed_parts[:GROUPS], feed_parts[GROUPS:]
    normed_slots = return_slots(normed_parts)
    from_core = shifted(sent, "dp", 1)
    residual_grad, branch_grad, residual_sums, *grad_slots = call(
        residual_kernel,
        [((TOKENS, WIDTH), f32), ((TOKENS, WIDTH), bf16), ((8, WIDTH), f32)]
        + [((GROUP_HEADS, 64, 128), bf16)] * GROUPS,
        smem=1,
        inputs=7,
        outside=1,
        scratch=[pltpu.VMEM((WIDTH, WIDTH), bf16), pltpu.SemaphoreType.DMA],
        micros=3,
    )(scalars, residual, *normed_slots, cotangent, params_rows, rest_copy)
    grad_slots = grad_slots[:1] + [
        shifted(grad_slots[by], "heads", by) for by in range(1, GROUPS)
    ]
    leaving = jnp.stack(grad_slots, axis=1).reshape(GROUP_HEADS * QUARTERS, 64, 128)
    leaving = jnp.concatenate([leaving, jnp.zeros((4, 64, 128), bf16)], axis=0)
    leaving, later_branch = lax.optimization_barrier((leaving, branch_grad))
    out_grads = lax.all_to_all(leaving, "blk", 0, 0, tiled=True)
    b_slots = gather_slots(later_branch)
    _, own_attended = lax.optimization_barrier((out_grads, own_attended))
    (rest_grad,) = call(rest_grad_kernel, [((BLOCKS, 64, WIDTH), bf16)], inputs=7, micros=3)(
        kept, from_core, own_attended, *b_slots
    )
    rest_grad, out_grads = lax.optimization_barrier((rest_grad, out_grads))
    rest_parts = lax.all_to_all(rest_grad, "blk", 0, 0, tiled=True)
    (leaving,) = call(
        attend_back_kernel,
        [((BLOCKS, 576, 128), bf16)],
        scratch=[
            pltpu.VMEM((128, QUERY_ROWS), bf16),
            pltpu.VMEM((128, QUERY_ROWS), bf16),
            pltpu.VMEM((QUERY_ROWS, 128), bf16),
            pltpu.VMEM((QUERY_ROWS, 128), bf16),
            pltpu.VMEM((BLOCKS, HEAD_DIM, BLOCK_ROWS), bf16),
            pltpu.VMEM((HEAD_DIM, QUERY_ROWS), f32),
            pltpu.VMEM((BLOCK_ROWS, TOKENS), f32),
        ],
        smem=1,
        inputs=4,
        micros=35,
    )(scalars, arrived, out_grads, attended_cols, log_total)
    leaving, rest_parts, output_parts, feed_sums, residual_sums = lax.optimization_barrier(
        (leaving, rest_parts, output_parts, feed_sums, residual_sums)
    )
    mixed_parts = lax.all_to_all(leaving, "blk", 0, 0, tiled=True)
    output_slots = return_slots(output_parts)
    output_slots, rest_parts, feed_sums, residual_sums = lax.optimization_barrier(
        (output_slots, rest_parts, feed_sums, residual_sums)
    )
    rest_sum = jnp.sum(rest_parts.astype(f32), axis=0)
    down_sum = rest_sum[0:24]
    first_core = scalars[2] == 0
    attn_kept = jnp.where(first_core, rest_sum[48:54], rest_sum[54:60])
    attn_sent = jnp.where(first_core, rest_sum[54:60], rest_sum[48:54])
    attn_sum = attn_kept + shifted(attn_sent, "dp", 1)
    up_sum = exchange_groups(rest_sum[24:48].reshape(GROUPS, 6, WIDTH))
    up_sum = up_sum.reshape(GROUPS, 6, 32, 24).transpose(1, 2, 0, 3).reshape(6, HIDDEN)

    at_group = (lax.iota(jnp.int32, GROUPS) == member).astype(f32)[:, None]
    early_terms = jnp.concatenate(
        [
            jnp.zeros((4, WIDTH), f32),
            residual_sums[0:1],
            feed_sums[0:2],
            residual_sums[1:2],
            (at_group[None] * feed_sums[2].reshape(32, 1, 24)).reshape(4, WIDTH),
            jnp.zeros((4, WIDTH), f32),
        ],
        axis=0,
    )
    qkv_grad, *normed_parts = call(
        mixed_back_kernel,
        [((WIDTH, 640), bf16)] + [((TOKENS, WIDTH), bf16)] * GROUPS,
        scratch=[pltpu.VMEM((16, WIDTH), f32)],
        smem=1,
        inputs=8,
    )(scalars, mixed_parts, *x_slots, params_rows, qkv_copy, early_terms)
    with jax.named_scope("qkv_terms"):
        came = lax.all_to_all(qkv_grad.reshape(OWNERS, 30, 128), EVERY, 0, 0, tiled=True)
        qkv_sum = jnp.sum(came.reshape(32, GROUPS, 30, 128).astype(f32), axis=0)
        qkv_sum = qkv_sum.reshape(GROUPS, 6, 640)
        vector_sum = jnp.sum(qkv_sum[:, :, 576:608], axis=0)
        vector_sum = (vector_sum[:, 0:12] + vector_sum[:, 16:28]).T
        pairs = qkv_sum[:, :, :384].reshape(GROUPS, 6, GROUP_HEADS, 2, HEAD_DIM)
        pairs = pairs.transpose(1, 3, 0, 2, 4).reshape(6, 2 * WIDTH)
        alone = qkv_sum[:, :, 384:576].transpose(1, 0, 2).reshape(6, WIDTH)
        qkv_sum = jnp.concatenate([alone, pairs], axis=1)
    normed_slots = return_slots(normed_parts)

    def summed(slots):
        slots = [slot.astype(f32) for slot in slots]
        return (slots[0] + slots[1]) + (slots[2] + slots[3])

    output = (residual + summed(output_slots) + params_rows[7]).astype(bf16)
    unit, inverse = unit_norm(inputs.astype(f32))
    input_grad = residual_grad + norm_backward(summed(normed_slots), unit, inverse, params_rows[0])

    qkv_updated, qkv_moment, qkv_squares = adam_step(
        qkv_weight, qkv_sum, qkv_first, qkv_second, 0.04, 1.0
    )
    attn_updated, attn_moment, attn_squares = adam_step(
        attn_weight, attn_sum, attn_first, attn_second, 0.1, 1.0
    )
    up_updated, up_moment, up_squares = adam_step(up_weight, up_sum, up_first, up_second, 0.03, 1.0)
    down_updated, down_moment, down_squares = adam_step(
        down_weight, down_sum, down_first, down_second, 0.02, 1.0
    )
    vector_updated, vector_moment, vector_squares = adam_step(
        vectors, vector_sum, vector_first, vector_second, 0.7, 0.0
    )
    return (
        output,
        input_grad,
        qkv_updated,
        attn_updated,
        up_updated,
        down_updated,
        vector_updated,
        qkv_moment,
        attn_moment,
        up_moment,
        down_moment,
        vector_moment,
        qkv_squares,
        attn_squares,
        up_squares,
        down_squares,
        vector_squares,
    )


def solution(mesh):
    rows, columns = P(EVERY, None), P(None, EVERY)
    weights = (rows, rows, rows, rows, columns)
    return jax.shard_map(
        per_device,
        mesh=mesh,
        in_specs=(rows, rows) + weights * 3,
        out_specs=(rows, rows) + weights * 3,
        check_vma=False,
    )
```

```python
import functools

import jax
import jax.numpy as jnp
from jax import lax
from jax.experimental import pallas as pl
from jax.experimental.pallas import tpu as pltpu
from jax.sharding import PartitionSpec as P

STEP = 10
WIDTH = 768
HIDDEN = 3072
HEAD_DIM = 64
GROUPS = 4
GROUP_HEADS = 3
GROUP_WIDTH = 192
BLOCKS = 16
QUARTERS = 4
TOKENS = 128
BLOCK_ROWS = 512
OWNERS = 128
QUERY_ROWS = BLOCKS * TOKENS
EVERY = ("dp", "blk", "heads")

norm_epsilon = 1e-05
first_decay = 0.9
second_decay = 0.95
adam_epsilon = 1e-08
weight_decay = 0.1
masked_score = -1e30
bf16 = jnp.bfloat16
f32 = jnp.float32


def shifted(array, axis, by):
    count = lax.axis_size(axis)
    return lax.ppermute(array, axis, [(i, (i + by) % count) for i in range(count)])


def gather_slots(array):
    return [array] + [shifted(array, "heads", by) for by in range(1, GROUPS)]


def return_slots(slots):
    return [slots[0]] + [shifted(slots[by], "heads", -by) for by in range(1, GROUPS)]


def exchange_groups(parts):
    member = lax.axis_index("heads")
    rolled = lax.dynamic_slice_in_dim(jnp.concatenate([parts, parts]), member, GROUPS, 0)
    got = [rolled[0]] + [shifted(rolled[by], "heads", by) for by in range(1, GROUPS)]
    turned = jnp.stack(got[::-1])
    return lax.dynamic_slice_in_dim(
        jnp.concatenate([turned, turned]), GROUPS - 1 - member, GROUPS, 0
    )


def dot(left, right, left_dim=1, right_dim=0):
    return lax.dot_general(
        left, right, (((left_dim,), (right_dim,)), ((), ())), preferred_element_type=f32
    )


def unit_norm(values):
    centred = values - jnp.mean(values, axis=-1, keepdims=True)
    variance = jnp.mean(centred * centred, axis=-1, keepdims=True)
    inverse = lax.rsqrt(variance + norm_epsilon)
    return centred * inverse, inverse


def norm_backward(grad_rows, unit_rows, inverse, gain):
    scaled = grad_rows * gain
    mean_grad = jnp.mean(scaled, axis=-1, keepdims=True)
    mean_unit = jnp.mean(scaled * unit_rows, axis=-1, keepdims=True)
    return inverse * (scaled - mean_grad - unit_rows * mean_unit)


def call(kernel, outs, scratch=(), smem=0, inputs=0, outside=0, micros=5):
    in_specs = [pl.BlockSpec(memory_space=pltpu.SMEM)] * smem + [
        pl.BlockSpec(memory_space=pltpu.VMEM)
    ] * inputs
    in_specs = in_specs + [pl.BlockSpec(memory_space=pl.ANY)] * outside
    return pl.pallas_call(
        kernel,
        out_shape=[jax.ShapeDtypeStruct(shape, dtype) for shape, dtype in outs],
        in_specs=in_specs,
        out_specs=[pl.BlockSpec(memory_space=pltpu.VMEM)] * len(outs),
        scratch_shapes=list(scratch),
        compiler_params=pltpu.CompilerParams(vmem_limit_bytes=56 * 2**20),
        cost_estimate=pl.CostEstimate(
            flops=micros * 10**9, bytes_accessed=2**20, transcendentals=0
        ),
    )


def fold_rows(rows):
    return jnp.concatenate([rows[:64], rows[64:]], axis=1)


def unfold_rows(folded):
    return jnp.concatenate([folded[:, :64], folded[:, 64:]], axis=0)


def project_kernel(scalars, x0, x1, x2, x3, own_half, other_half, out, params, weight):
    half = WIDTH // 2
    core = scalars[2]
    weight[pl.ds(pl.multiple_of(core * half, half), half)] = own_half[...]
    weight[pl.ds(pl.multiple_of((1 - core) * half, half), half)] = other_half[...]
    params[...] = transposed(weight[:, 576:640])[0:16]
    rows = jnp.concatenate([x0[...], x1[...], x2[...], x3[...]], axis=0).astype(f32)
    unit, _ = unit_norm(rows)
    normed = (unit * params[0:1] + params[1:2]).astype(bf16)
    own = jnp.zeros((2, GROUP_WIDTH), f32)
    for group in range(GROUPS):
        part = params[2:4, group * GROUP_WIDTH : (group + 1) * GROUP_WIDTH]
        own = own + jnp.where(scalars[0] == group, part, 0.0)
    pieces = []
    for head in range(GROUP_HEADS):
        pieces.append(jnp.zeros((1, HEAD_DIM), f32))
        pieces.append(own[1:2, head * HEAD_DIM : (head + 1) * HEAD_DIM])
    bias = jnp.concatenate(pieces + [own[0:1]], axis=1)
    mixed = (dot(normed, weight[:, 0:576]) + bias).astype(bf16)
    for head in range(GROUP_HEADS):
        pair = mixed[:, head * 128 : (head + 1) * 128]
        first = 384 + head * HEAD_DIM
        queries = mixed[:, first : first + HEAD_DIM]
        for quarter in range(QUARTERS):
            place = head * QUARTERS + quarter
            out[place, 0:BLOCK_ROWS] = pair
            out[place, BLOCK_ROWS:] = fold_rows(queries[quarter * TOKENS : (quarter + 1) * TOKENS])
    out[GROUP_HEADS * QUARTERS :] = jnp.zeros((BLOCKS - GROUP_HEADS * QUARTERS, 576, 128), bf16)


def place_gap(scalars):
    member, quarter = scalars[0], scalars[1]
    key_row = lax.broadcasted_iota(jnp.int32, (BLOCK_ROWS, TOKENS), 0)
    query_row = lax.broadcasted_iota(jnp.int32, (BLOCK_ROWS, TOKENS), 1)
    key_sub = (member - key_row // TOKENS + GROUPS) & (GROUPS - 1)
    query_sub = (member - quarter + GROUPS) & (GROUPS - 1)
    return (query_sub - key_sub) * TOKENS + query_row - (key_row & (TOKENS - 1))


def mask_lead(scores, allowed):
    masked = jnp.where(allowed, scores[:, :TOKENS], masked_score)
    if scores.shape[1] == TOKENS:
        return masked
    return jnp.concatenate([masked, scores[:, TOKENS:]], axis=1)


def transposed(values):
    return jnp.transpose(values.astype(f32), (1, 0))


def attend_kernel(
    scalars, arrived, out, out_cols, log_total, query_cols, value_cols, gap, peak, total
):
    gap[...] = place_gap(scalars).astype(f32)
    for block in range(BLOCKS):
        queries = unfold_rows(arrived[block, BLOCK_ROWS:])
        query_cols[:, block * TOKENS : (block + 1) * TOKENS] = (
            transposed(queries) * 0.125
        ).astype(bf16)
        value_cols[block, 0:64] = transposed(arrived[block, 0:BLOCK_ROWS])[64:128].astype(bf16)
        value_cols[block, 64:80] = jnp.ones((16, BLOCK_ROWS), bf16)
    peak[...] = jnp.full((1, QUERY_ROWS), masked_score, f32)
    total[...] = jnp.zeros((80, QUERY_ROWS), f32)
    for block in range(BLOCKS):
        first = block * TOKENS
        scores = dot(arrived[block, 0:BLOCK_ROWS, 0:64], query_cols[:, first:])
        scores = mask_lead(scores, gap[...] >= 0.0)
        old = peak[:, first:]
        new = jnp.maximum(old, jnp.max(scores, axis=0, keepdims=True))
        weights = jnp.exp(scores - new).astype(bf16)
        total[:, first:] = total[:, first:] * jnp.exp(old - new) + dot(value_cols[block], weights)
        peak[:, first:] = new
    row_total = total[64:65]
    out_cols[...] = total[0:64] / row_total
    log_total[...] = peak[...] + jnp.log(row_total)
    for block in range(BLOCKS):
        attended = out_cols[:, block * TOKENS : (block + 1) * TOKENS]
        out[block] = fold_rows(transposed(attended).astype(bf16))


def split_three(values):
    high = values.astype(bf16)
    rest = values - high.astype(f32)
    middle = rest.astype(bf16)
    low = (rest - middle.astype(f32)).astype(bf16)
    return high, middle, low


def attend_back_kernel(
    scalars,
    arrived,
    grads,
    out_cols,
    log_total,
    out,
    query_cols,
    grad_cols,
    query_rows,
    grad_rows,
    key_cols,
    query_total,
    gap,
):
    gap[...] = place_gap(scalars).astype(f32)
    key_lane = lax.broadcasted_iota(jnp.int32, (BLOCK_ROWS, 128), 1)
    lane_row = lax.broadcasted_iota(jnp.int32, (64, TOKENS), 0)
    zeros = jnp.zeros((TOKENS, 64), bf16)

    def part_rows(values):
        parts = [part.astype(f32) for part in split_three(values)]
        rows = jnp.where(lane_row == 2, parts[2], 0.0)
        rows = jnp.where(lane_row == 1, parts[1], rows)
        return jnp.where(lane_row == 0, parts[0], rows).astype(bf16)

    for block in range(BLOCKS):
        here = slice(block * TOKENS, (block + 1) * TOKENS)
        queries = unfold_rows(arrived[block, BLOCK_ROWS:]) * 0.125
        query_rows[here] = jnp.concatenate([queries, zeros], axis=1)
        query_cols[0:64, here] = transposed(queries).astype(bf16)
        query_cols[64:128, here] = part_rows(-log_total[:, here])
        out_grad = unfold_rows(grads[block])
        grad_rows[here] = jnp.concatenate([zeros, out_grad], axis=1)
        grad_col = transposed(out_grad)
        grad_cols[64:128, here] = grad_col.astype(bf16)
        delta = jnp.sum(grad_col * out_cols[:, here], axis=0, keepdims=True)
        grad_cols[0:64, here] = part_rows(-delta)
        key_cols[block] = transposed(arrived[block, 0:BLOCK_ROWS])[0:64].astype(bf16)
    query_total[...] = jnp.zeros((64, QUERY_ROWS), f32)
    for block in range(BLOCKS):
        first = block * TOKENS
        pair = arrived[block, 0:BLOCK_ROWS]
        keys = jnp.where(key_lane < 64, pair, jnp.where(key_lane < 67, 1.0, 0.0).astype(bf16))
        values = jnp.where(key_lane >= 64, pair, jnp.where(key_lane < 3, 1.0, 0.0).astype(bf16))
        scores = dot(keys, query_cols[:, first:])
        weights = jnp.exp(mask_lead(scores, gap[...] >= 0.0))
        score_grad = (weights * dot(values, grad_cols[:, first:])).astype(bf16)
        out[block, 0:BLOCK_ROWS] = (
            dot(score_grad, query_rows[first:]) + dot(weights.astype(bf16), grad_rows[first:])
        ).astype(bf16)
        query_total[:, first:] += dot(key_cols[block], score_grad)
    for block in range(BLOCKS):
        here = slice(block * TOKENS, (block + 1) * TOKENS)
        out[block, BLOCK_ROWS:] = fold_rows(
            transposed(query_total[:, here] * 0.125).astype(bf16)
        )


def store_slots(outs, values):
    for slot, out in enumerate(outs):
        out[...] = values[slot * TOKENS : (slot + 1) * TOKENS]


def feed_kernel(
    scalars,
    x0,
    x1,
    x2,
    x3,
    a0,
    a1,
    a2,
    a3,
    c0,
    c1,
    c2,
    c3,
    weights,
    params,
    bias,
    residual_out,
    own_attended,
    kept,
    sent,
    sums,
    *parts,
):
    *parts, both = parts
    output_parts, normed_parts = parts[:GROUPS], parts[GROUPS:]
    member = scalars[0]
    residual = jnp.concatenate([x0[...], x1[...], x2[...], x3[...]], axis=0).astype(f32)
    residual = residual + params[4:5]
    select_row = lax.broadcasted_iota(jnp.int32, (GROUP_WIDTH, GROUP_WIDTH), 0)
    select_col = lax.broadcasted_iota(jnp.int32, (GROUP_WIDTH, GROUP_WIDTH), 1)
    wanted = (select_col // 6) * 24 + member * 6 + select_col % 6
    own = jnp.zeros((BLOCK_ROWS, GROUP_WIDTH), f32)
    for group, arrived in enumerate((a0, a1, a2, a3)):
        slots = []
        for slot in range(QUARTERS):
            quarter = (slot - group) % QUARTERS
            slots.append(
                jnp.concatenate(
                    [unfold_rows(arrived[head * QUARTERS + quarter]) for head in range(GROUP_HEADS)],
                    axis=1,
                )
            )
        attended = jnp.concatenate(slots, axis=0)
        first = ((member - group + GROUPS) & (GROUPS - 1)) * GROUP_WIDTH
        rows = pl.ds(pl.multiple_of(first, 64), GROUP_WIDTH)
        residual = residual + dot(attended, weights[rows, WIDTH : 2 * WIDTH])
        chosen = jnp.where(select_row + first == wanted, 1.0, 0.0).astype(bf16)
        own = own + dot(attended, chosen)
    own_attended[...] = own.astype(bf16)
    residual_out[...] = residual[0:TOKENS]
    unit, _ = unit_norm(residual)
    normed = (unit * params[5:6] + params[6:7]).astype(bf16)
    pre = dot(normed, weights[:, 0:WIDTH]) + bias[...]
    slope = 0.7978845608028654
    tanh = jnp.tanh(slope * (pre + 0.044715 * pre * pre * pre))
    hidden = (0.5 * pre * (1.0 + tanh)).astype(bf16)
    store_slots(output_parts, dot(hidden, weights[:, 2 * WIDTH :]).astype(bf16))
    cotangent = jnp.concatenate([c0[...], c1[...], c2[...], c3[...]], axis=0)
    hidden_grad = dot(cotangent, weights[:, 2 * WIDTH :], 1, 1)
    pull = 0.5 * (1.0 + tanh) + 0.5 * pre * (1.0 - tanh * tanh) * slope * (
        1.0 + 3.0 * 0.044715 * pre * pre
    )
    pre_grad = (hidden_grad * pull).astype(bf16)
    down = dot(hidden, cotangent, 0, 0).reshape(32, 24, WIDTH)
    up = dot(normed, pre_grad, 0, 0).reshape(32, 24, WIDTH)
    both[...] = jnp.concatenate([down, up], axis=1).astype(bf16)
    core = scalars[2]
    kept[...] = both[pl.ds(core * BLOCKS, BLOCKS)]
    sent[...] = both[pl.ds((1 - core) * BLOCKS, BLOCKS)]
    normed_grad = dot(pre_grad, weights[:, 0:WIDTH], 1, 1)
    store_slots(normed_parts, normed_grad.astype(bf16))
    sums[0:1] = jnp.sum(normed_grad * unit, axis=0, keepdims=True)
    sums[1:2] = jnp.sum(normed_grad, axis=0, keepdims=True)
    sums[2:3] = jnp.sum(pre_grad.astype(f32), axis=0, keepdims=True)
    sums[3:8] = jnp.zeros((5, WIDTH), f32)


def residual_kernel(
    scalars,
    residual,
    p0,
    p1,
    p2,
    p3,
    cotangent,
    params,
    weights,
    grad_out,
    branch_out,
    sums,
    d0,
    d1,
    d2,
    d3,
    attn_weight,
    copied,
):
    copy = pltpu.make_async_copy(weights.at[:, pl.ds(WIDTH, WIDTH)], attn_weight, copied)
    copy.start()
    normed_grad = (p0[...].astype(f32) + p1[...].astype(f32)) + (
        p2[...].astype(f32) + p3[...].astype(f32)
    )
    unit, inverse = unit_norm(residual[...])
    grad_rows = cotangent[...].astype(f32)
    residual_grad = grad_rows + norm_backward(normed_grad, unit, inverse, params[5:6])
    grad_out[...] = residual_grad
    branch_grad = residual_grad.astype(bf16)
    branch_out[...] = branch_grad
    sums[0:1] = jnp.sum(branch_grad.astype(f32), axis=0, keepdims=True)
    sums[1:2] = jnp.sum(grad_rows, axis=0, keepdims=True)
    sums[2:8] = jnp.zeros((6, WIDTH), f32)
    copy.wait()
    for group, out in enumerate((d0, d1, d2, d3)):
        first = ((scalars[0] + group) & (GROUPS - 1)) * GROUP_WIDTH
        rows = pl.ds(pl.multiple_of(first, 64), GROUP_WIDTH)
        attended_grad = dot(branch_grad, attn_weight[rows], 1, 1).astype(bf16)
        for head in range(GROUP_HEADS):
            out[head] = fold_rows(attended_grad[:, head * HEAD_DIM : (head + 1) * HEAD_DIM])


def rest_grad_kernel(kept, came, own_attended, b0, b1, b2, b3, out):
    branch_grad = jnp.concatenate([b0[...], b1[...], b2[...], b3[...]], axis=0)
    attn = dot(own_attended[...], branch_grad, 0, 0).reshape(2, BLOCKS, 6, WIDTH)
    feed = kept[...].astype(f32) + came[...].astype(f32)
    empty = jnp.zeros((BLOCKS, 4, WIDTH), f32)
    out[...] = jnp.concatenate([feed, attn[0], attn[1], empty], axis=1).astype(bf16)


def mixed_back_kernel(
    scalars,
    arrived,
    x0,
    x1,
    x2,
    x3,
    params,
    weight,
    early_terms,
    kept,
    sent,
    p0,
    p1,
    p2,
    p3,
    vector_terms,
    both,
):
    rows = jnp.concatenate([x0[...], x1[...], x2[...], x3[...]], axis=0).astype(f32)
    unit, _ = unit_norm(rows)
    normed = (unit * params[0:1] + params[1:2]).astype(bf16)
    pieces, queries = [], []
    for head in range(GROUP_HEADS):
        pair = jnp.zeros((BLOCK_ROWS, 128), f32)
        for quarter in range(QUARTERS):
            pair = pair + arrived[head * QUARTERS + quarter, 0:BLOCK_ROWS].astype(f32)
        pieces.append(pair.astype(bf16))
        queries.append(
            jnp.concatenate(
                [
                    unfold_rows(arrived[head * QUARTERS + quarter, BLOCK_ROWS:])
                    for quarter in range(QUARTERS)
                ],
                axis=0,
            )
        )
    mixed_grad = jnp.concatenate(pieces + queries, axis=1)
    normed_grad = dot(mixed_grad, weight[:, 0:576], 1, 1)
    store_slots((p0, p1, p2, p3), normed_grad.astype(bf16))
    column_sums = jnp.sum(mixed_grad.astype(f32), axis=0, keepdims=True)
    value_sums = jnp.concatenate(
        [column_sums[:, head * 128 + 64 : head * 128 + 128] for head in range(GROUP_HEADS)], axis=1
    )
    lane = lax.broadcasted_iota(jnp.int32, (1, WIDTH), 1)
    first = scalars[0] * GROUP_WIDTH
    own = (lane >= first) & (lane < first + GROUP_WIDTH)
    vector_terms[...] = early_terms[...]
    vector_terms[0:1] = jnp.sum(normed_grad * unit, axis=0, keepdims=True)
    vector_terms[1:2] = jnp.sum(normed_grad, axis=0, keepdims=True)
    vector_terms[2:3] = jnp.where(own, jnp.concatenate([column_sums[:, 384:]] * GROUPS, axis=1), 0.0)
    vector_terms[3:4] = jnp.where(own, jnp.concatenate([value_sums] * GROUPS, axis=1), 0.0)
    high = vector_terms[...].astype(bf16).astype(f32)
    low = vector_terms[...] - high
    columns = transposed(jnp.concatenate([high, low, jnp.zeros((32, WIDTH), f32)], axis=0))
    weight_grad = jnp.concatenate([dot(normed, mixed_grad, 0, 0), columns], axis=1)
    both[...] = weight_grad.reshape(OWNERS, 6, 640)
    half = OWNERS // 2
    core = scalars[2]
    kept[...] = both[pl.ds(core * half, half)]
    sent[...] = both[pl.ds((1 - core) * half, half)].astype(bf16)


def adam_step(weight, gradient, first, second, rate, decay_flag):
    moment = first_decay * first + (1.0 - first_decay) * gradient
    squares = second_decay * second + (1.0 - second_decay) * gradient * gradient
    fix_one = 1.0 - first_decay**STEP
    fix_two = 1.0 - second_decay**STEP
    direction = moment / fix_one / (jnp.sqrt(squares / fix_two) + adam_epsilon)
    updated = weight - rate * (direction + decay_flag * weight_decay * weight)
    return (updated, moment, squares)


def per_device(
    inputs,
    cotangent,
    qkv_weight,
    attn_weight,
    up_weight,
    down_weight,
    vectors,
    qkv_first,
    attn_first,
    up_first,
    down_first,
    vector_first,
    qkv_second,
    attn_second,
    up_second,
    down_second,
    vector_second,
):
    member = lax.axis_index("heads")
    scalars = jnp.stack(
        [member, lax.axis_index("blk") % QUARTERS, lax.axis_index("dp")]
    ).astype(jnp.int32)

    with jax.named_scope("qkv_copies"):
        by_head = qkv_weight.astype(bf16).reshape(6, 3, GROUPS, GROUP_HEADS, HEAD_DIM)
        pairs = by_head[:, 1:].transpose(2, 0, 3, 1, 4).reshape(GROUPS, 6, 384)
        alone = by_head[:, 0].transpose(1, 0, 2, 3).reshape(GROUPS, 6, GROUP_WIDTH)
        vector_cols = jnp.broadcast_to(vectors.astype(bf16).T[None], (GROUPS, 6, 12))
        leaving = jnp.concatenate(
            [pairs, alone, vector_cols, jnp.zeros((GROUPS, 6, 52), bf16)], axis=2
        )
        leaving = jnp.broadcast_to(leaving[None], (BLOCKS, GROUPS, 6, 640)).reshape(64, 6, 640)
        leaving, later_inputs, later_up, later_attn = lax.optimization_barrier(
            (leaving, inputs, up_weight, attn_weight)
        )
        came = lax.all_to_all(leaving, ("blk", "heads"), 0, 0, tiled=True)
        x_slots = gather_slots(later_inputs)
        up_parts = later_up.astype(bf16).reshape(6, 32, GROUPS, 24).transpose(2, 0, 1, 3)
        up_parts = up_parts.reshape(GROUPS, 6, WIDTH)
        attn_parts = jnp.broadcast_to(later_attn.astype(bf16)[None], (GROUPS, 6, WIDTH))
        other_parts = exchange_groups(jnp.concatenate([up_parts, attn_parts], axis=2))
        came, x_slots, other_parts = lax.optimization_barrier((came, x_slots, other_parts))
        own_half = came.reshape(WIDTH // 2, 640)
        other_half = shifted(own_half, "dp", 1)
    leaving, params_rows, qkv_copy = call(
        project_kernel,
        [((BLOCKS, 576, 128), bf16), ((16, WIDTH), f32), ((WIDTH, 640), bf16)],
        smem=1,
        inputs=6,
    )(scalars, *x_slots, own_half, other_half)

    leaving, later_cotangent = lax.optimization_barrier((leaving, cotangent))
    arrived = lax.all_to_all(leaving, "blk", 0, 0, tiled=True)
    with jax.named_scope("other_copies"):
        came = other_parts.reshape(24, 2 * WIDTH)
        rest = jnp.concatenate([came, down_weight.astype(bf16)], axis=1)
        rest_copy = lax.all_gather(rest, ("dp", "blk"), axis=0, tiled=True)
    c_slots = gather_slots(later_cotangent)
    arrived, c_slots = lax.optimization_barrier((arrived, c_slots))
    hidden_bias = lax.dynamic_slice_in_dim(
        params_rows[8:12].reshape(32, GROUPS, 24), member, 1, 1
    )
    hidden_bias = hidden_bias.reshape(1, WIDTH)

    attended, attended_cols, log_total = call(
        attend_kernel,
        [
            ((BLOCKS, 64, 128), bf16),
            ((HEAD_DIM, QUERY_ROWS), f32),
            ((1, QUERY_ROWS), f32),
        ],
        scratch=[
            pltpu.VMEM((HEAD_DIM, QUERY_ROWS), bf16),
            pltpu.VMEM((BLOCKS, 80, BLOCK_ROWS), bf16),
            pltpu.VMEM((BLOCK_ROWS, TOKENS), f32),
            pltpu.VMEM((1, QUERY_ROWS), f32),
            pltpu.VMEM((80, QUERY_ROWS), f32),
        ],
        smem=1,
        inputs=1,
        micros=50,
    )(scalars, arrived)
    attended = lax.all_to_all(attended, "blk", 0, 0, tiled=True)
    a_slots = gather_slots(attended[: GROUP_HEADS * QUARTERS])
    (
        residual,
        own_attended,
        kept,
        sent,
        feed_sums,
        *feed_parts,
    ) = call(
        feed_kernel,
        [
            ((TOKENS, WIDTH), f32),
            ((BLOCK_ROWS, GROUP_WIDTH), bf16),
            ((BLOCKS, 48, WIDTH), bf16),
            ((BLOCKS, 48, WIDTH), bf16),
            ((8, WIDTH), f32),
        ]
        + [((TOKENS, WIDTH), bf16)] * (2 * GROUPS),
        smem=1,
        inputs=15,
        scratch=[pltpu.VMEM((2 * BLOCKS, 48, WIDTH), bf16)],
        micros=10,
    )(scalars, *x_slots, *a_slots, *c_slots, rest_copy, params_rows, hidden_bias)

    output_parts, normed_parts = feed_parts[:GROUPS], feed_parts[GROUPS:]
    normed_slots = return_slots(normed_parts)
    from_core = shifted(sent, "dp", 1)
    residual_grad, branch_grad, residual_sums, *grad_slots = call(
        residual_kernel,
        [((TOKENS, WIDTH), f32), ((TOKENS, WIDTH), bf16), ((8, WIDTH), f32)]
        + [((GROUP_HEADS, 64, 128), bf16)] * GROUPS,
        smem=1,
        inputs=7,
        outside=1,
        scratch=[pltpu.VMEM((WIDTH, WIDTH), bf16), pltpu.SemaphoreType.DMA],
        micros=3,
    )(scalars, residual, *normed_slots, cotangent, params_rows, rest_copy)
    grad_slots = grad_slots[:1] + [
        shifted(grad_slots[by], "heads", by) for by in range(1, GROUPS)
    ]
    leaving = jnp.stack(grad_slots, axis=1).reshape(GROUP_HEADS * QUARTERS, 64, 128)
    leaving = jnp.concatenate([leaving, jnp.zeros((4, 64, 128), bf16)], axis=0)
    leaving, later_branch = lax.optimization_barrier((leaving, branch_grad))
    out_grads = lax.all_to_all(leaving, "blk", 0, 0, tiled=True)
    b_slots = gather_slots(later_branch)
    _, own_attended = lax.optimization_barrier((out_grads, own_attended))
    (rest_grad,) = call(rest_grad_kernel, [((BLOCKS, 64, WIDTH), bf16)], inputs=7, micros=3)(
        kept, from_core, own_attended, *b_slots
    )
    rest_grad, out_grads = lax.optimization_barrier((rest_grad, out_grads))
    rest_parts = lax.all_to_all(rest_grad, "blk", 0, 0, tiled=True)
    (leaving,) = call(
        attend_back_kernel,
        [((BLOCKS, 576, 128), bf16)],
        scratch=[
            pltpu.VMEM((128, QUERY_ROWS), bf16),
            pltpu.VMEM((128, QUERY_ROWS), bf16),
            pltpu.VMEM((QUERY_ROWS, 128), bf16),
            pltpu.VMEM((QUERY_ROWS, 128), bf16),
            pltpu.VMEM((BLOCKS, HEAD_DIM, BLOCK_ROWS), bf16),
            pltpu.VMEM((HEAD_DIM, QUERY_ROWS), f32),
            pltpu.VMEM((BLOCK_ROWS, TOKENS), f32),
        ],
        smem=1,
        inputs=4,
        micros=35,
    )(scalars, arrived, out_grads, attended_cols, log_total)
    leaving, rest_parts = lax.optimization_barrier((leaving, rest_parts))
    mixed_parts = lax.all_to_all(leaving, "blk", 0, 0, tiled=True)
    rest_sum = jnp.sum(rest_parts.astype(f32), axis=0)
    down_sum = rest_sum[0:24]
    first_core = scalars[2] == 0
    attn_kept = jnp.where(first_core, rest_sum[48:54], rest_sum[54:60])
    attn_sent = jnp.where(first_core, rest_sum[54:60], rest_sum[48:54])
    attn_sum = attn_kept + shifted(attn_sent, "dp", 1)
    attn_sum, rest_sum, output_parts, feed_sums, residual_sums = lax.optimization_barrier(
        (attn_sum, rest_sum, output_parts, feed_sums, residual_sums)
    )
    output_slots = return_slots(output_parts)
    output_slots, rest_sum, feed_sums, residual_sums = lax.optimization_barrier(
        (output_slots, rest_sum, feed_sums, residual_sums)
    )
    up_sum = exchange_groups(rest_sum[24:48].reshape(GROUPS, 6, WIDTH))
    up_sum = up_sum.reshape(GROUPS, 6, 32, 24).transpose(1, 2, 0, 3).reshape(6, HIDDEN)

    at_group = (lax.iota(jnp.int32, GROUPS) == member).astype(f32)[:, None]
    early_terms = jnp.concatenate(
        [
            jnp.zeros((4, WIDTH), f32),
            residual_sums[0:1],
            feed_sums[0:2],
            residual_sums[1:2],
            (at_group[None] * feed_sums[2].reshape(32, 1, 24)).reshape(4, WIDTH),
            jnp.zeros((4, WIDTH), f32),
        ],
        axis=0,
    )
    kept, sent, *normed_parts = call(
        mixed_back_kernel,
        [((64, 6, 640), f32), ((64, 6, 640), bf16)] + [((TOKENS, WIDTH), bf16)] * GROUPS,
        scratch=[pltpu.VMEM((16, WIDTH), f32), pltpu.VMEM((OWNERS, 6, 640), f32)],
        smem=1,
        inputs=8,
    )(scalars, mixed_parts, *x_slots, params_rows, qkv_copy, early_terms)
    with jax.named_scope("qkv_terms"):
        qkv_grad = (kept + shifted(sent, "dp", 1).astype(f32)).astype(bf16)
        came = lax.all_to_all(qkv_grad, ("blk", "heads"), 0, 0, tiled=True)
        qkv_sum = jnp.sum(came.reshape(BLOCKS, GROUPS, 6, 640).astype(f32), axis=0)
        vector_sum = jnp.sum(qkv_sum[:, :, 576:608], axis=0)
        vector_sum = (vector_sum[:, 0:12] + vector_sum[:, 16:28]).T
        pairs = qkv_sum[:, :, :384].reshape(GROUPS, 6, GROUP_HEADS, 2, HEAD_DIM)
        pairs = pairs.transpose(1, 3, 0, 2, 4).reshape(6, 2 * WIDTH)
        alone = qkv_sum[:, :, 384:576].transpose(1, 0, 2).reshape(6, WIDTH)
        qkv_sum = jnp.concatenate([alone, pairs], axis=1)
    _, normed_slots = lax.optimization_barrier((came, return_slots(normed_parts)))

    def summed(slots):
        slots = [slot.astype(f32) for slot in slots]
        return (slots[0] + slots[1]) + (slots[2] + slots[3])

    output = (residual + summed(output_slots) + params_rows[7]).astype(bf16)
    unit, inverse = unit_norm(inputs.astype(f32))
    input_grad = residual_grad + norm_backward(summed(normed_slots), unit, inverse, params_rows[0])

    qkv_updated, qkv_moment, qkv_squares = adam_step(
        qkv_weight, qkv_sum, qkv_first, qkv_second, 0.04, 1.0
    )
    attn_updated, attn_moment, attn_squares = adam_step(
        attn_weight, attn_sum, attn_first, attn_second, 0.1, 1.0
    )
    up_updated, up_moment, up_squares = adam_step(up_weight, up_sum, up_first, up_second, 0.03, 1.0)
    down_updated, down_moment, down_squares = adam_step(
        down_weight, down_sum, down_first, down_second, 0.02, 1.0
    )
    vector_updated, vector_moment, vector_squares = adam_step(
        vectors, vector_sum, vector_first, vector_second, 0.7, 0.0
    )
    return (
        output,
        input_grad,
        qkv_updated,
        attn_updated,
        up_updated,
        down_updated,
        vector_updated,
        qkv_moment,
        attn_moment,
        up_moment,
        down_moment,
        vector_moment,
        qkv_squares,
        attn_squares,
        up_squares,
        down_squares,
        vector_squares,
    )


def solution(mesh):
    rows, columns = P(EVERY, None), P(None, EVERY)
    weights = (rows, rows, rows, rows, columns)
    return jax.shard_map(
        per_device,
        mesh=mesh,
        in_specs=(rows, rows) + weights * 3,
        out_specs=(rows, rows) + weights * 3,
        check_vma=False,
    )
```

```python
import functools

import jax
import jax.numpy as jnp
from jax import lax
from jax.experimental import pallas as pl
from jax.experimental.pallas import tpu as pltpu
from jax.sharding import PartitionSpec as P

STEP = 10
WIDTH = 768
HIDDEN = 3072
HEAD_DIM = 64
GROUPS = 4
GROUP_HEADS = 3
GROUP_WIDTH = 192
BLOCKS = 16
QUARTERS = 4
TOKENS = 128
BLOCK_ROWS = 512
OWNERS = 128
QUERY_ROWS = BLOCKS * TOKENS
EVERY = ("dp", "blk", "heads")

norm_epsilon = 1e-05
first_decay = 0.9
second_decay = 0.95
adam_epsilon = 1e-08
weight_decay = 0.1
masked_score = -1e30
bf16 = jnp.bfloat16
f32 = jnp.float32


def shifted(array, axis, by):
    count = lax.axis_size(axis)
    return lax.ppermute(array, axis, [(i, (i + by) % count) for i in range(count)])


def gather_slots(array):
    return [array] + [shifted(array, "heads", by) for by in range(1, GROUPS)]


def return_slots(slots):
    return [slots[0]] + [shifted(slots[by], "heads", -by) for by in range(1, GROUPS)]


def exchange_groups(parts):
    member = lax.axis_index("heads")
    rolled = lax.dynamic_slice_in_dim(jnp.concatenate([parts, parts]), member, GROUPS, 0)
    got = [rolled[0]] + [shifted(rolled[by], "heads", by) for by in range(1, GROUPS)]
    turned = jnp.stack(got[::-1])
    return lax.dynamic_slice_in_dim(
        jnp.concatenate([turned, turned]), GROUPS - 1 - member, GROUPS, 0
    )


def dot(left, right, left_dim=1, right_dim=0):
    return lax.dot_general(
        left, right, (((left_dim,), (right_dim,)), ((), ())), preferred_element_type=f32
    )


def unit_norm(values):
    centred = values - jnp.mean(values, axis=-1, keepdims=True)
    variance = jnp.mean(centred * centred, axis=-1, keepdims=True)
    inverse = lax.rsqrt(variance + norm_epsilon)
    return centred * inverse, inverse


def norm_backward(grad_rows, unit_rows, inverse, gain):
    scaled = grad_rows * gain
    mean_grad = jnp.mean(scaled, axis=-1, keepdims=True)
    mean_unit = jnp.mean(scaled * unit_rows, axis=-1, keepdims=True)
    return inverse * (scaled - mean_grad - unit_rows * mean_unit)


def call(kernel, outs, scratch=(), smem=0, inputs=0, outside=0, micros=5):
    in_specs = [pl.BlockSpec(memory_space=pltpu.SMEM)] * smem + [
        pl.BlockSpec(memory_space=pltpu.VMEM)
    ] * inputs
    in_specs = in_specs + [pl.BlockSpec(memory_space=pl.ANY)] * outside
    return pl.pallas_call(
        kernel,
        out_shape=[jax.ShapeDtypeStruct(shape, dtype) for shape, dtype in outs],
        in_specs=in_specs,
        out_specs=[pl.BlockSpec(memory_space=pltpu.VMEM)] * len(outs),
        scratch_shapes=list(scratch),
        compiler_params=pltpu.CompilerParams(vmem_limit_bytes=56 * 2**20),
        cost_estimate=pl.CostEstimate(
            flops=micros * 10**9, bytes_accessed=2**20, transcendentals=0
        ),
    )


def fold_rows(rows):
    return jnp.concatenate([rows[:64], rows[64:]], axis=1)


def unfold_rows(folded):
    return jnp.concatenate([folded[:, :64], folded[:, 64:]], axis=0)


def project_kernel(scalars, x0, x1, x2, x3, own_half, other_half, out, params, weight):
    half = WIDTH // 2
    core = scalars[2]
    weight[pl.ds(pl.multiple_of(core * half, half), half)] = own_half[...]
    weight[pl.ds(pl.multiple_of((1 - core) * half, half), half)] = other_half[...]
    params[...] = transposed(weight[:, 576:640])[0:16]
    rows = jnp.concatenate([x0[...], x1[...], x2[...], x3[...]], axis=0).astype(f32)
    unit, _ = unit_norm(rows)
    normed = (unit * params[0:1] + params[1:2]).astype(bf16)
    own = jnp.zeros((2, GROUP_WIDTH), f32)
    for group in range(GROUPS):
        part = params[2:4, group * GROUP_WIDTH : (group + 1) * GROUP_WIDTH]
        own = own + jnp.where(scalars[0] == group, part, 0.0)
    pieces = []
    for head in range(GROUP_HEADS):
        pieces.append(jnp.zeros((1, HEAD_DIM), f32))
        pieces.append(own[1:2, head * HEAD_DIM : (head + 1) * HEAD_DIM])
    bias = jnp.concatenate(pieces + [own[0:1]], axis=1)
    mixed = (dot(normed, weight[:, 0:576]) + bias).astype(bf16)
    for head in range(GROUP_HEADS):
        pair = mixed[:, head * 128 : (head + 1) * 128]
        first = 384 + head * HEAD_DIM
        queries = mixed[:, first : first + HEAD_DIM]
        for quarter in range(QUARTERS):
            place = head * QUARTERS + quarter
            out[place, 0:BLOCK_ROWS] = pair
            out[place, BLOCK_ROWS:] = fold_rows(queries[quarter * TOKENS : (quarter + 1) * TOKENS])
    out[GROUP_HEADS * QUARTERS :] = jnp.zeros((BLOCKS - GROUP_HEADS * QUARTERS, 576, 128), bf16)


def place_gap(scalars):
    member, quarter = scalars[0], scalars[1]
    key_row = lax.broadcasted_iota(jnp.int32, (BLOCK_ROWS, TOKENS), 0)
    query_row = lax.broadcasted_iota(jnp.int32, (BLOCK_ROWS, TOKENS), 1)
    key_sub = (member - key_row // TOKENS + GROUPS) & (GROUPS - 1)
    query_sub = (member - quarter + GROUPS) & (GROUPS - 1)
    return (query_sub - key_sub) * TOKENS + query_row - (key_row & (TOKENS - 1))


def mask_lead(scores, allowed):
    masked = jnp.where(allowed, scores[:, :TOKENS], masked_score)
    if scores.shape[1] == TOKENS:
        return masked
    return jnp.concatenate([masked, scores[:, TOKENS:]], axis=1)


def transposed(values):
    return jnp.transpose(values.astype(f32), (1, 0))


def attend_kernel(
    scalars, arrived, out, out_cols, log_total, query_cols, value_cols, gap, peak, total
):
    gap[...] = place_gap(scalars).astype(f32)
    for block in range(BLOCKS):
        queries = unfold_rows(arrived[block, BLOCK_ROWS:])
        query_cols[:, block * TOKENS : (block + 1) * TOKENS] = (
            transposed(queries) * 0.125
        ).astype(bf16)
        value_cols[block, 0:64] = transposed(arrived[block, 0:BLOCK_ROWS])[64:128].astype(bf16)
        value_cols[block, 64:80] = jnp.ones((16, BLOCK_ROWS), bf16)
    peak[...] = jnp.full((1, QUERY_ROWS), masked_score, f32)
    total[...] = jnp.zeros((80, QUERY_ROWS), f32)
    for block in range(BLOCKS):
        first = block * TOKENS
        scores = dot(arrived[block, 0:BLOCK_ROWS, 0:64], query_cols[:, first:])
        scores = mask_lead(scores, gap[...] >= 0.0)
        old = peak[:, first:]
        new = jnp.maximum(old, jnp.max(scores, axis=0, keepdims=True))
        weights = jnp.exp(scores - new).astype(bf16)
        total[:, first:] = total[:, first:] * jnp.exp(old - new) + dot(value_cols[block], weights)
        peak[:, first:] = new
    row_total = total[64:65]
    out_cols[...] = total[0:64] / row_total
    log_total[...] = peak[...] + jnp.log(row_total)
    for block in range(BLOCKS):
        attended = out_cols[:, block * TOKENS : (block + 1) * TOKENS]
        out[block] = fold_rows(transposed(attended).astype(bf16))


def split_three(values):
    high = values.astype(bf16)
    rest = values - high.astype(f32)
    middle = rest.astype(bf16)
    low = (rest - middle.astype(f32)).astype(bf16)
    return high, middle, low


def attend_back_kernel(
    scalars,
    arrived,
    grads,
    out_cols,
    log_total,
    out,
    query_cols,
    grad_cols,
    query_rows,
    grad_rows,
    key_cols,
    query_total,
    gap,
):
    gap[...] = place_gap(scalars).astype(f32)
    key_lane = lax.broadcasted_iota(jnp.int32, (BLOCK_ROWS, 128), 1)
    lane_row = lax.broadcasted_iota(jnp.int32, (64, TOKENS), 0)
    zeros = jnp.zeros((TOKENS, 64), bf16)

    def part_rows(values):
        parts = [part.astype(f32) for part in split_three(values)]
        rows = jnp.where(lane_row == 2, parts[2], 0.0)
        rows = jnp.where(lane_row == 1, parts[1], rows)
        return jnp.where(lane_row == 0, parts[0], rows).astype(bf16)

    for block in range(BLOCKS):
        here = slice(block * TOKENS, (block + 1) * TOKENS)
        queries = unfold_rows(arrived[block, BLOCK_ROWS:]) * 0.125
        query_rows[here] = jnp.concatenate([queries, zeros], axis=1)
        query_cols[0:64, here] = transposed(queries).astype(bf16)
        query_cols[64:128, here] = part_rows(-log_total[:, here])
        out_grad = unfold_rows(grads[block])
        grad_rows[here] = jnp.concatenate([zeros, out_grad], axis=1)
        grad_col = transposed(out_grad)
        grad_cols[64:128, here] = grad_col.astype(bf16)
        delta = jnp.sum(grad_col * out_cols[:, here], axis=0, keepdims=True)
        grad_cols[0:64, here] = part_rows(-delta)
        key_cols[block] = transposed(arrived[block, 0:BLOCK_ROWS])[0:64].astype(bf16)
    query_total[...] = jnp.zeros((64, QUERY_ROWS), f32)
    for block in range(BLOCKS):
        first = block * TOKENS
        pair = arrived[block, 0:BLOCK_ROWS]
        keys = jnp.where(key_lane < 64, pair, jnp.where(key_lane < 67, 1.0, 0.0).astype(bf16))
        values = jnp.where(key_lane >= 64, pair, jnp.where(key_lane < 3, 1.0, 0.0).astype(bf16))
        scores = dot(keys, query_cols[:, first:])
        weights = jnp.exp(mask_lead(scores, gap[...] >= 0.0))
        score_grad = (weights * dot(values, grad_cols[:, first:])).astype(bf16)
        out[block, 0:BLOCK_ROWS] = (
            dot(score_grad, query_rows[first:]) + dot(weights.astype(bf16), grad_rows[first:])
        ).astype(bf16)
        query_total[:, first:] += dot(key_cols[block], score_grad)
    for block in range(BLOCKS):
        here = slice(block * TOKENS, (block + 1) * TOKENS)
        out[block, BLOCK_ROWS:] = fold_rows(
            transposed(query_total[:, here] * 0.125).astype(bf16)
        )


def store_slots(outs, values):
    for slot, out in enumerate(outs):
        out[...] = values[slot * TOKENS : (slot + 1) * TOKENS]


def feed_kernel(
    scalars,
    x0,
    x1,
    x2,
    x3,
    a0,
    a1,
    a2,
    a3,
    c0,
    c1,
    c2,
    c3,
    weights,
    params,
    bias,
    residual_out,
    own_attended,
    kept,
    sent,
    sums,
    *parts,
):
    *parts, both = parts
    output_parts, normed_parts = parts[:GROUPS], parts[GROUPS:]
    member = scalars[0]
    residual = jnp.concatenate([x0[...], x1[...], x2[...], x3[...]], axis=0).astype(f32)
    residual = residual + params[4:5]
    select_row = lax.broadcasted_iota(jnp.int32, (GROUP_WIDTH, GROUP_WIDTH), 0)
    select_col = lax.broadcasted_iota(jnp.int32, (GROUP_WIDTH, GROUP_WIDTH), 1)
    wanted = (select_col // 6) * 24 + member * 6 + select_col % 6
    own = jnp.zeros((BLOCK_ROWS, GROUP_WIDTH), f32)
    for group, arrived in enumerate((a0, a1, a2, a3)):
        slots = []
        for slot in range(QUARTERS):
            quarter = (slot - group) % QUARTERS
            slots.append(
                jnp.concatenate(
                    [unfold_rows(arrived[head * QUARTERS + quarter]) for head in range(GROUP_HEADS)],
                    axis=1,
                )
            )
        attended = jnp.concatenate(slots, axis=0)
        first = ((member - group + GROUPS) & (GROUPS - 1)) * GROUP_WIDTH
        rows = pl.ds(pl.multiple_of(first, 64), GROUP_WIDTH)
        residual = residual + dot(attended, weights[rows, WIDTH : 2 * WIDTH])
        chosen = jnp.where(select_row + first == wanted, 1.0, 0.0).astype(bf16)
        own = own + dot(attended, chosen)
    own_attended[...] = own.astype(bf16)
    residual_out[...] = residual[0:TOKENS]
    unit, _ = unit_norm(residual)
    normed = (unit * params[5:6] + params[6:7]).astype(bf16)
    pre = dot(normed, weights[:, 0:WIDTH]) + bias[...]
    slope = 0.7978845608028654
    tanh = jnp.tanh(slope * (pre + 0.044715 * pre * pre * pre))
    hidden = (0.5 * pre * (1.0 + tanh)).astype(bf16)
    store_slots(output_parts, dot(hidden, weights[:, 2 * WIDTH :]).astype(bf16))
    cotangent = jnp.concatenate([c0[...], c1[...], c2[...], c3[...]], axis=0)
    hidden_grad = dot(cotangent, weights[:, 2 * WIDTH :], 1, 1)
    pull = 0.5 * (1.0 + tanh) + 0.5 * pre * (1.0 - tanh * tanh) * slope * (
        1.0 + 3.0 * 0.044715 * pre * pre
    )
    pre_grad = (hidden_grad * pull).astype(bf16)
    down = dot(hidden, cotangent, 0, 0).reshape(32, 24, WIDTH)
    up = dot(normed, pre_grad, 0, 0).reshape(32, 24, WIDTH)
    both[...] = jnp.concatenate([down, up], axis=1).astype(bf16)
    core = scalars[2]
    kept[...] = both[pl.ds(core * BLOCKS, BLOCKS)]
    sent[...] = both[pl.ds((1 - core) * BLOCKS, BLOCKS)]
    normed_grad = dot(pre_grad, weights[:, 0:WIDTH], 1, 1)
    store_slots(normed_parts, normed_grad.astype(bf16))
    sums[0:1] = jnp.sum(normed_grad * unit, axis=0, keepdims=True)
    sums[1:2] = jnp.sum(normed_grad, axis=0, keepdims=True)
    sums[2:3] = jnp.sum(pre_grad.astype(f32), axis=0, keepdims=True)
    sums[3:8] = jnp.zeros((5, WIDTH), f32)


def residual_kernel(
    scalars,
    residual,
    p0,
    p1,
    p2,
    p3,
    cotangent,
    params,
    weights,
    grad_out,
    branch_out,
    sums,
    d0,
    d1,
    d2,
    d3,
    attn_weight,
    copied,
):
    copy = pltpu.make_async_copy(weights.at[:, pl.ds(WIDTH, WIDTH)], attn_weight, copied)
    copy.start()
    normed_grad = (p0[...].astype(f32) + p1[...].astype(f32)) + (
        p2[...].astype(f32) + p3[...].astype(f32)
    )
    unit, inverse = unit_norm(residual[...])
    grad_rows = cotangent[...].astype(f32)
    residual_grad = grad_rows + norm_backward(normed_grad, unit, inverse, params[5:6])
    grad_out[...] = residual_grad
    branch_grad = residual_grad.astype(bf16)
    branch_out[...] = branch_grad
    sums[0:1] = jnp.sum(branch_grad.astype(f32), axis=0, keepdims=True)
    sums[1:2] = jnp.sum(grad_rows, axis=0, keepdims=True)
    sums[2:8] = jnp.zeros((6, WIDTH), f32)
    copy.wait()
    for group, out in enumerate((d0, d1, d2, d3)):
        first = ((scalars[0] + group) & (GROUPS - 1)) * GROUP_WIDTH
        rows = pl.ds(pl.multiple_of(first, 64), GROUP_WIDTH)
        attended_grad = dot(branch_grad, attn_weight[rows], 1, 1).astype(bf16)
        for head in range(GROUP_HEADS):
            out[head] = fold_rows(attended_grad[:, head * HEAD_DIM : (head + 1) * HEAD_DIM])


def rest_grad_kernel(kept, came, own_attended, b0, b1, b2, b3, out):
    branch_grad = jnp.concatenate([b0[...], b1[...], b2[...], b3[...]], axis=0)
    attn = dot(own_attended[...], branch_grad, 0, 0).reshape(2, BLOCKS, 6, WIDTH)
    feed = kept[...].astype(f32) + came[...].astype(f32)
    empty = jnp.zeros((BLOCKS, 4, WIDTH), f32)
    out[...] = jnp.concatenate([feed, attn[0], attn[1], empty], axis=1).astype(bf16)


def mixed_back_kernel(
    scalars,
    arrived,
    x0,
    x1,
    x2,
    x3,
    params,
    weight,
    early_terms,
    kept,
    sent,
    p0,
    p1,
    p2,
    p3,
    vector_terms,
    both,
):
    rows = jnp.concatenate([x0[...], x1[...], x2[...], x3[...]], axis=0).astype(f32)
    unit, _ = unit_norm(rows)
    normed = (unit * params[0:1] + params[1:2]).astype(bf16)
    pieces, queries = [], []
    for head in range(GROUP_HEADS):
        pair = jnp.zeros((BLOCK_ROWS, 128), f32)
        for quarter in range(QUARTERS):
            pair = pair + arrived[head * QUARTERS + quarter, 0:BLOCK_ROWS].astype(f32)
        pieces.append(pair.astype(bf16))
        queries.append(
            jnp.concatenate(
                [
                    unfold_rows(arrived[head * QUARTERS + quarter, BLOCK_ROWS:])
                    for quarter in range(QUARTERS)
                ],
                axis=0,
            )
        )
    mixed_grad = jnp.concatenate(pieces + queries, axis=1)
    normed_grad = dot(mixed_grad, weight[:, 0:576], 1, 1)
    store_slots((p0, p1, p2, p3), normed_grad.astype(bf16))
    column_sums = jnp.sum(mixed_grad.astype(f32), axis=0, keepdims=True)
    value_sums = jnp.concatenate(
        [column_sums[:, head * 128 + 64 : head * 128 + 128] for head in range(GROUP_HEADS)], axis=1
    )
    lane = lax.broadcasted_iota(jnp.int32, (1, WIDTH), 1)
    first = scalars[0] * GROUP_WIDTH
    own = (lane >= first) & (lane < first + GROUP_WIDTH)
    vector_terms[...] = early_terms[...]
    vector_terms[0:1] = jnp.sum(normed_grad * unit, axis=0, keepdims=True)
    vector_terms[1:2] = jnp.sum(normed_grad, axis=0, keepdims=True)
    vector_terms[2:3] = jnp.where(own, jnp.concatenate([column_sums[:, 384:]] * GROUPS, axis=1), 0.0)
    vector_terms[3:4] = jnp.where(own, jnp.concatenate([value_sums] * GROUPS, axis=1), 0.0)
    high = vector_terms[...].astype(bf16).astype(f32)
    low = vector_terms[...] - high
    columns = transposed(jnp.concatenate([high, low, jnp.zeros((32, WIDTH), f32)], axis=0))
    weight_grad = jnp.concatenate([dot(normed, mixed_grad, 0, 0), columns], axis=1)
    both[...] = weight_grad.reshape(OWNERS, 6, 640)
    half = OWNERS // 2
    core = scalars[2]
    kept[...] = both[pl.ds(core * half, half)]
    sent[...] = both[pl.ds((1 - core) * half, half)].astype(bf16)


def adam_step(weight, gradient, first, second, rate, decay_flag):
    moment = first_decay * first + (1.0 - first_decay) * gradient
    squares = second_decay * second + (1.0 - second_decay) * gradient * gradient
    fix_one = 1.0 - first_decay**STEP
    fix_two = 1.0 - second_decay**STEP
    direction = moment / fix_one / (jnp.sqrt(squares / fix_two) + adam_epsilon)
    updated = weight - rate * (direction + decay_flag * weight_decay * weight)
    return (updated, moment, squares)


def per_device(
    inputs,
    cotangent,
    qkv_weight,
    attn_weight,
    up_weight,
    down_weight,
    vectors,
    qkv_first,
    attn_first,
    up_first,
    down_first,
    vector_first,
    qkv_second,
    attn_second,
    up_second,
    down_second,
    vector_second,
):
    member = lax.axis_index("heads")
    scalars = jnp.stack(
        [member, lax.axis_index("blk") % QUARTERS, lax.axis_index("dp")]
    ).astype(jnp.int32)

    with jax.named_scope("qkv_copies"):
        by_head = qkv_weight.astype(bf16).reshape(6, 3, GROUPS, GROUP_HEADS, HEAD_DIM)
        pairs = by_head[:, 1:].transpose(2, 0, 3, 1, 4).reshape(GROUPS, 6, 384)
        alone = by_head[:, 0].transpose(1, 0, 2, 3).reshape(GROUPS, 6, GROUP_WIDTH)
        vector_cols = jnp.broadcast_to(vectors.astype(bf16).T[None], (GROUPS, 6, 12))
        leaving = jnp.concatenate(
            [pairs, alone, vector_cols, jnp.zeros((GROUPS, 6, 52), bf16)], axis=2
        )
        leaving = jnp.broadcast_to(leaving[None], (BLOCKS, GROUPS, 6, 640)).reshape(64, 6, 640)
        leaving, later_inputs, later_up, later_attn = lax.optimization_barrier(
            (leaving, inputs, up_weight, attn_weight)
        )
        came = lax.all_to_all(leaving, ("blk", "heads"), 0, 0, tiled=True)
        x_slots = gather_slots(later_inputs)
        up_parts = later_up.astype(bf16).reshape(6, 32, GROUPS, 24).transpose(2, 0, 1, 3)
        up_parts = up_parts.reshape(GROUPS, 6, WIDTH)
        attn_parts = jnp.broadcast_to(later_attn.astype(bf16)[None], (GROUPS, 6, WIDTH))
        other_parts = exchange_groups(jnp.concatenate([up_parts, attn_parts], axis=2))
        came, x_slots, other_parts = lax.optimization_barrier((came, x_slots, other_parts))
        own_half = came.reshape(WIDTH // 2, 640)
        other_half = shifted(own_half, "dp", 1)
    leaving, params_rows, qkv_copy = call(
        project_kernel,
        [((BLOCKS, 576, 128), bf16), ((16, WIDTH), f32), ((WIDTH, 640), bf16)],
        smem=1,
        inputs=6,
    )(scalars, *x_slots, own_half, other_half)

    leaving, later_cotangent = lax.optimization_barrier((leaving, cotangent))
    arrived = lax.all_to_all(leaving, "blk", 0, 0, tiled=True)
    with jax.named_scope("other_copies"):
        came = other_parts.reshape(24, 2 * WIDTH)
        rest = jnp.concatenate([came, down_weight.astype(bf16)], axis=1)
        rest_copy = lax.all_gather(rest, ("dp", "blk"), axis=0, tiled=True)
    c_slots = gather_slots(later_cotangent)
    arrived, c_slots = lax.optimization_barrier((arrived, c_slots))
    hidden_bias = lax.dynamic_slice_in_dim(
        params_rows[8:12].reshape(32, GROUPS, 24), member, 1, 1
    )
    hidden_bias = hidden_bias.reshape(1, WIDTH)

    attended, attended_cols, log_total = call(
        attend_kernel,
        [
            ((BLOCKS, 64, 128), bf16),
            ((HEAD_DIM, QUERY_ROWS), f32),
            ((1, QUERY_ROWS), f32),
        ],
        scratch=[
            pltpu.VMEM((HEAD_DIM, QUERY_ROWS), bf16),
            pltpu.VMEM((BLOCKS, 80, BLOCK_ROWS), bf16),
            pltpu.VMEM((BLOCK_ROWS, TOKENS), f32),
            pltpu.VMEM((1, QUERY_ROWS), f32),
            pltpu.VMEM((80, QUERY_ROWS), f32),
        ],
        smem=1,
        inputs=1,
        micros=50,
    )(scalars, arrived)
    attended = lax.all_to_all(attended, "blk", 0, 0, tiled=True)
    a_slots = gather_slots(attended[: GROUP_HEADS * QUARTERS])
    (
        residual,
        own_attended,
        kept,
        sent,
        feed_sums,
        *feed_parts,
    ) = call(
        feed_kernel,
        [
            ((TOKENS, WIDTH), f32),
            ((BLOCK_ROWS, GROUP_WIDTH), bf16),
            ((BLOCKS, 48, WIDTH), bf16),
            ((BLOCKS, 48, WIDTH), bf16),
            ((8, WIDTH), f32),
        ]
        + [((TOKENS, WIDTH), bf16)] * (2 * GROUPS),
        smem=1,
        inputs=15,
        scratch=[pltpu.VMEM((2 * BLOCKS, 48, WIDTH), bf16)],
        micros=10,
    )(scalars, *x_slots, *a_slots, *c_slots, rest_copy, params_rows, hidden_bias)

    output_parts, normed_parts = feed_parts[:GROUPS], feed_parts[GROUPS:]
    normed_slots = return_slots(normed_parts)
    from_core = shifted(sent, "dp", 1)
    residual_grad, branch_grad, residual_sums, *grad_slots = call(
        residual_kernel,
        [((TOKENS, WIDTH), f32), ((TOKENS, WIDTH), bf16), ((8, WIDTH), f32)]
        + [((GROUP_HEADS, 64, 128), bf16)] * GROUPS,
        smem=1,
        inputs=7,
        outside=1,
        scratch=[pltpu.VMEM((WIDTH, WIDTH), bf16), pltpu.SemaphoreType.DMA],
        micros=3,
    )(scalars, residual, *normed_slots, cotangent, params_rows, rest_copy)
    grad_slots = grad_slots[:1] + [
        shifted(grad_slots[by], "heads", by) for by in range(1, GROUPS)
    ]
    leaving = jnp.stack(grad_slots, axis=1).reshape(GROUP_HEADS * QUARTERS, 64, 128)
    leaving = jnp.concatenate([leaving, jnp.zeros((4, 64, 128), bf16)], axis=0)
    leaving, later_branch = lax.optimization_barrier((leaving, branch_grad))
    out_grads = lax.all_to_all(leaving, "blk", 0, 0, tiled=True)
    b_slots = gather_slots(later_branch)
    _, own_attended = lax.optimization_barrier((out_grads, own_attended))
    (rest_grad,) = call(rest_grad_kernel, [((BLOCKS, 64, WIDTH), bf16)], inputs=7, micros=3)(
        kept, from_core, own_attended, *b_slots
    )
    rest_grad, out_grads = lax.optimization_barrier((rest_grad, out_grads))
    rest_parts = lax.all_to_all(rest_grad, "blk", 0, 0, tiled=True)
    (leaving,) = call(
        attend_back_kernel,
        [((BLOCKS, 576, 128), bf16)],
        scratch=[
            pltpu.VMEM((128, QUERY_ROWS), bf16),
            pltpu.VMEM((128, QUERY_ROWS), bf16),
            pltpu.VMEM((QUERY_ROWS, 128), bf16),
            pltpu.VMEM((QUERY_ROWS, 128), bf16),
            pltpu.VMEM((BLOCKS, HEAD_DIM, BLOCK_ROWS), bf16),
            pltpu.VMEM((HEAD_DIM, QUERY_ROWS), f32),
            pltpu.VMEM((BLOCK_ROWS, TOKENS), f32),
        ],
        smem=1,
        inputs=4,
        micros=35,
    )(scalars, arrived, out_grads, attended_cols, log_total)
    leaving, rest_parts = lax.optimization_barrier((leaving, rest_parts))
    mixed_parts = lax.all_to_all(leaving, "blk", 0, 0, tiled=True)
    rest_sum = jnp.sum(rest_parts.astype(f32), axis=0)
    down_sum = rest_sum[0:24]
    first_core = scalars[2] == 0
    attn_kept = jnp.where(first_core, rest_sum[48:54], rest_sum[54:60])
    attn_sent = jnp.where(first_core, rest_sum[54:60], rest_sum[48:54])
    attn_sum = attn_kept + shifted(attn_sent, "dp", 1)
    attn_sum, rest_sum, output_parts, feed_sums, residual_sums = lax.optimization_barrier(
        (attn_sum, rest_sum, output_parts, feed_sums, residual_sums)
    )
    output_slots = return_slots(output_parts)
    output_slots, rest_sum, feed_sums, residual_sums = lax.optimization_barrier(
        (output_slots, rest_sum, feed_sums, residual_sums)
    )
    up_sum = exchange_groups(rest_sum[24:48].reshape(GROUPS, 6, WIDTH))
    up_sum = up_sum.reshape(GROUPS, 6, 32, 24).transpose(1, 2, 0, 3).reshape(6, HIDDEN)

    at_group = (lax.iota(jnp.int32, GROUPS) == member).astype(f32)[:, None]
    early_terms = jnp.concatenate(
        [
            jnp.zeros((4, WIDTH), f32),
            residual_sums[0:1],
            feed_sums[0:2],
            residual_sums[1:2],
            (at_group[None] * feed_sums[2].reshape(32, 1, 24)).reshape(4, WIDTH),
            jnp.zeros((4, WIDTH), f32),
        ],
        axis=0,
    )
    kept, sent, *normed_parts = call(
        mixed_back_kernel,
        [((64, 6, 640), f32), ((64, 6, 640), bf16)] + [((TOKENS, WIDTH), bf16)] * GROUPS,
        scratch=[pltpu.VMEM((16, WIDTH), f32), pltpu.VMEM((OWNERS, 6, 640), f32)],
        smem=1,
        inputs=8,
    )(scalars, mixed_parts, *x_slots, params_rows, qkv_copy, early_terms)
    with jax.named_scope("qkv_terms"):
        normed_slots = return_slots(normed_parts)
        from_core, normed_slots[1], normed_slots[3] = lax.optimization_barrier(
            (shifted(sent, "dp", 1), normed_slots[1], normed_slots[3])
        )
        qkv_grad = (kept + from_core.astype(f32)).astype(bf16)
        came = lax.all_to_all(qkv_grad, ("blk", "heads"), 0, 0, tiled=True)
        qkv_sum = jnp.sum(came.reshape(BLOCKS, GROUPS, 6, 640).astype(f32), axis=0)
        vector_sum = jnp.sum(qkv_sum[:, :, 576:608], axis=0)
        vector_sum = (vector_sum[:, 0:12] + vector_sum[:, 16:28]).T
        pairs = qkv_sum[:, :, :384].reshape(GROUPS, 6, GROUP_HEADS, 2, HEAD_DIM)
        pairs = pairs.transpose(1, 3, 0, 2, 4).reshape(6, 2 * WIDTH)
        alone = qkv_sum[:, :, 384:576].transpose(1, 0, 2).reshape(6, WIDTH)
        qkv_sum = jnp.concatenate([alone, pairs], axis=1)
    _, normed_slots = lax.optimization_barrier((came, normed_slots))

    def summed(slots):
        slots = [slot.astype(f32) for slot in slots]
        return (slots[0] + slots[1]) + (slots[2] + slots[3])

    output = (residual + summed(output_slots) + params_rows[7]).astype(bf16)
    unit, inverse = unit_norm(inputs.astype(f32))
    input_grad = residual_grad + norm_backward(summed(normed_slots), unit, inverse, params_rows[0])

    qkv_updated, qkv_moment, qkv_squares = adam_step(
        qkv_weight, qkv_sum, qkv_first, qkv_second, 0.04, 1.0
    )
    attn_updated, attn_moment, attn_squares = adam_step(
        attn_weight, attn_sum, attn_first, attn_second, 0.1, 1.0
    )
    up_updated, up_moment, up_squares = adam_step(up_weight, up_sum, up_first, up_second, 0.03, 1.0)
    down_updated, down_moment, down_squares = adam_step(
        down_weight, down_sum, down_first, down_second, 0.02, 1.0
    )
    vector_updated, vector_moment, vector_squares = adam_step(
        vectors, vector_sum, vector_first, vector_second, 0.7, 0.0
    )
    return (
        output,
        input_grad,
        qkv_updated,
        attn_updated,
        up_updated,
        down_updated,
        vector_updated,
        qkv_moment,
        attn_moment,
        up_moment,
        down_moment,
        vector_moment,
        qkv_squares,
        attn_squares,
        up_squares,
        down_squares,
        vector_squares,
    )


def solution(mesh):
    rows, columns = P(EVERY, None), P(None, EVERY)
    weights = (rows, rows, rows, rows, columns)
    return jax.shard_map(
        per_device,
        mesh=mesh,
        in_specs=(rows, rows) + weights * 3,
        out_specs=(rows, rows) + weights * 3,
        check_vma=False,
    )
```
